32 devices in a mesh: ctx: 8 (over z, x), dp: 4 (over y, core).
Axes of the slice: x: 2, y: 2, z: 4, core: 2. Of those that a mesh axis runs over, the one named last changes fastest.
Arguments:
- tokens: bfloat16 [4, 2048, 768], P('dp', 'ctx'), may hold values from -6 to 6
- cotangent: bfloat16 [4, 2048, 768], P('dp', 'ctx'), may hold values from -6 to 6
- w_query: bfloat16 [768, 768], P('dp'), may hold values from -0.21875 to 0.21875
- w_key: bfloat16 [768, 768], P('dp'), may hold values from -0.21875 to 0.21875
- w_value: bfloat16 [768, 768], P('dp'), may hold values from -0.21875 to 0.21875
- attention_output_weight: bfloat16 [768, 768], P('dp'), may hold values from -3.5 to 3.5
- router: bfloat16 [768, 4], P('dp'), may hold values from -0.15917969 to 0.15917969
- norm1_gain: bfloat16 [768], P('dp'), may hold values from 0.5 to 1.5
- norm2_gain: bfloat16 [768], P('dp'), may hold values from 0.5 to 1.5
- attn_bias: bfloat16 [32, 12], P('dp'), may hold values from -4 to 4
- w_in: bfloat16 [4, 768, 3072], P('dp', None, 'ctx'), may hold values from -0.21875 to 0.21875
- w_out: bfloat16 [4, 3072, 768], P('dp', 'ctx'), may hold values from -0.109375 to 0.109375
- routes: int32 [4, 2048, 2], P('dp', 'ctx'), may hold values from 0 to 3, all different within a row; in each aligned block of 256 rows (0 to 255, 256 to 511, ..., all dimensions but the last counted through in order) at most 256 rows name the same one
- buckets: int32 [2048], replicated, may hold values from 0 to 31
Outputs:
- layer_out: bfloat16 [4, 2048, 768], P('dp', 'ctx')
- input_grad: float32 [4, 2048, 768], P('dp', 'ctx')
- grad_w_query: float32 [768, 768], P('dp')
- grad_w_key: float32 [768, 768], P('dp')
- grad_w_value: float32 [768, 768], P('dp')
- grad_w_output: float32 [768, 768], P('dp')
- grad_router: float32 [768, 4], P('dp')
- grad_norm1_gain: float32 [768], P('dp')
- grad_norm2_gain: float32 [768], P('dp')
- grad_attn_bias: float32 [32, 12], P('dp')
- grad_w_in: float32 [4, 768, 3072], P('dp', None, 'ctx')
- grad_w_out: float32 [4, 3072, 768], P('dp', 'ctx')
The draws below stay inside these ranges and needn't reach their ends.
Inputs may be any that keep to these rules, and one draw needn't show every extreme that they name: `routes`: the 2 experts of a token differ. Among the tokens of one device (aligned blocks of 256 tokens of a sequence), no expert is named more than 256 times, a bound that some block reaches.
All inputs are finite; a program needn't handle non-finite values.
Results may differ from the reference program's by a relative error of at most 0.02.
Values may be sent and summed in bfloat16 or wider, within the bound.
No kernel may reach another device: no remote copies, remote signals or barrier semaphores. Data moves between devices by JAX's collectives and lax.ppermute only.
A program may use at most 128 MiB of HBM per device.

```python
import math
import jax
import jax.numpy as jnp
import numpy as np
from jax import lax

D = 768
HEADS = 12
HEAD_DIM = 64
FF = 3072
TOP = 2
NB = 32
TOK_DEV = 256
SEQ_LEN = 2048
SEQS = 4
EXPERTS = 4
CAP = 256
N_CTX = 8


def with_ends(array, stream_key, least, top_value):
    shape = array.shape
    place = [jax.random.randint(jax.random.fold_in(stream_key, axis), (), 0, shape[axis]) for axis in range(len(shape))]
    array = array.at[tuple(place)].set(least)
    longest = shape.index(max(shape))
    place[longest] = (place[longest] + 1) % shape[longest]
    return array.at[tuple(place)].set(top_value)


def steps_of(stream_key, extent, shards, smallest, top_value):
    def one(axis_at, shards_of):
        draws = jax.random.uniform(jax.random.fold_in(jax.random.fold_in(stream_key, 6), axis_at), (shards_of,), jnp.float32, smallest / len(shards), top_value / len(shards))
        return jnp.repeat(jnp.exp(draws), extent[axis_at] // shards_of).reshape((-1,) + (1,) * (len(extent) - axis_at - 1))

    factor_of = one(*shards[0])
    for cut in shards[1:]:
        factor_of = factor_of * one(*cut)
    return factor_of


def assign_block(own_key, own, number, rows, number_of, top, limit, lean):
    ranking = jax.random.permutation(own_key, number_of)
    heavy_load, ordinary = load_shares(number_of, rows * top, limit, lean, True), load_shares(number_of, rows * top, limit, lean, False)
    places = jnp.arange(number_of)

    def named(lengths, offset_by):
        used = int((lengths > 0).sum())
        fixed = max(1, used // 4)
        moved = fixed + (places - fixed + offset_by * (used - fixed)) % max(1, number_of - fixed)
        return jnp.zeros((number_of,), jnp.int32).at[ranking[jnp.where(places < fixed, places, moved)]].set(jnp.asarray(lengths, jnp.int32))

    lengths = jnp.where(number % 4 == 0, named(heavy_load, number // 4), named(ordinary, number - number // 4 - 1))
    mixed = jax.random.permutation(jax.random.fold_in(own, 3), number_of)
    giver, sink = mixed[0:number_of // 2 * 2:2], mixed[1:number_of // 2 * 2:2]
    margin = jnp.minimum(lengths[giver] - 1, limit - lengths[sink]) // 2
    margin = jnp.where((giver == ranking[0]) | (sink == ranking[0]) | (lengths[sink] == 0), 0, jnp.maximum(margin, 0))
    moved = jax.random.randint(jax.random.fold_in(own, 4), (number_of // 2,), 0, 1 << 20) % (margin + 1)
    lengths = lengths.at[giver].add(-moved).at[sink].add(moved)
    members = jnp.searchsorted(jnp.cumsum(lengths), jnp.arange(rows * top), side="right").astype(jnp.int32)
    listing = members.reshape(top, rows).T
    listing = listing[jax.random.permutation(jax.random.fold_in(own, 1), rows)]
    offset_by = jax.random.randint(jax.random.fold_in(own, 2), (rows, 1), 0, top)
    return jnp.take_along_axis(listing, (jnp.arange(top)[None, :] + offset_by) % top, axis=1)


def load_shares(count, total, reach, slope, full):
    portions = [(1 << 20) // math.isqrt(standing ** slope) + 1 for standing in range(1, count + 1)]
    largest = reach if full else min(reach, max(-(-total // count), total * portions[0] // sum(portions)))
    least = 1 if total - largest >= count - 1 else 0
    counts, rest = [largest] + [least] * (count - 1), total - largest - least * (count - 1)
    while rest > 0:
        free = [i for i in range(1, count) if counts[i] < largest] or [i for i in range(1, count) if counts[i] < reach]
        pool, left = sum([portions[i] for i in free]), rest
        for i in free:
            more = min(reach - counts[i], max(1, left * portions[i] // pool), rest)
            counts[i] = counts[i] + more
            rest = rest - more
    return np.array(counts)


def bell_draw(own_key, dims, deviation, most, shards=(), held_as=jnp.bfloat16):
    drawn = deviation * jax.random.normal(own_key, dims, jnp.float32)
    if shards:
        drawn = drawn * steps_of(own_key, dims, shards, -0.22, 0.18)
    return jnp.clip(drawn, -most, most).astype(held_as)


def setup_inputs(seed: int = 0) -> dict:
    streams_of = jax.random.split(jax.random.key(seed), 15)
    tokens = bell_draw(streams_of[0], (SEQS, SEQ_LEN, D), 1.0, 6.0, ((0, 4), (1, 8)))
    cotangent = bell_draw(streams_of[1], (SEQS, SEQ_LEN, D), 1.0, 6.0, ((0, 4), (1, 8)))
    w_query = bell_draw(streams_of[2], (D, D), D ** -0.5, 0.21875, ((0, 4),))
    w_key = bell_draw(streams_of[3], (D, D), D ** -0.5, 0.21875, ((0, 4),))
    w_value = bell_draw(streams_of[4], (D, D), D ** -0.5, 0.21875, ((0, 4),))
    attention_output_weight = bell_draw(streams_of[5], (D, D), 3 ** -0.5, 3.5, ((0, 4),))
    router = bell_draw(streams_of[6], (D, EXPERTS), 0.027, 0.15917969, ((0, 4),))
    norm1_gain = jnp.clip(1.0 + 0.1 * jax.random.normal(streams_of[7], (D,), jnp.float32), 0.5, 1.5).astype(jnp.bfloat16)
    norm2_gain = jnp.clip(1.0 + 0.1 * jax.random.normal(streams_of[8], (D,), jnp.float32), 0.5, 1.5).astype(jnp.bfloat16)
    attn_bias = bell_draw(streams_of[9], (NB, HEADS), 1.0, 4.0, ((0, 4),))
    w_in = bell_draw(streams_of[10], (EXPERTS, D, FF), D ** -0.5, 0.21875, ((0, 4), (2, 8)))
    w_out = bell_draw(streams_of[11], (EXPERTS, FF, D), FF ** -0.5, 0.109375, ((0, 4), (1, 8)))
    routes_keys = jax.random.split(jax.random.fold_in(streams_of[12], 1), SEQS * SEQ_LEN // TOK_DEV)
    routes_turns = jax.random.permutation(jax.random.fold_in(streams_of[12], 3), SEQS * SEQ_LEN // TOK_DEV)
    routes = jax.vmap(lambda own, number: assign_block(jax.random.fold_in(streams_of[12], 2), own, number, TOK_DEV, EXPERTS, TOP, CAP, 1))(routes_keys, routes_turns).reshape((SEQS, SEQ_LEN, TOP))
    buckets = with_ends(jax.random.randint(streams_of[13], (SEQ_LEN,), 0, NB), jax.random.fold_in(streams_of[13], 1), 0, NB - 1).astype(jnp.int32)
    return dict(tokens=tokens, cotangent=cotangent, w_query=w_query, w_key=w_key, w_value=w_value, attention_output_weight=attention_output_weight, router=router, norm1_gain=norm1_gain, norm2_gain=norm2_gain, attn_bias=attn_bias, w_in=w_in, w_out=w_out, routes=routes, buckets=buckets)


highest_score = lax.Precision.HIGHEST
eps_norm = 1e-06
masked_score = -1e+30

@jax.custom_vjp
def lowest_pass(v):
    return lax.optimization_barrier(v.astype(jnp.bfloat16)).astype(jnp.float32)

@jax.custom_vjp
def lowest_backward(v):
    return v

def low_keep(v):
    return (lowest_pass(v), None)

def low_pass(kept, grad):
    return (grad,)

def back_keep(v):
    return (v, None)

def back_low(kept, grad):
    return (lowest_pass(grad),)
lowest_pass.defvjp(low_keep, low_pass)
lowest_backward.defvjp(back_keep, back_low)

def rms_scale(inputs, gain):
    return inputs * lax.rsqrt(lax.optimization_barrier(jnp.mean(inputs * inputs, axis=-1, keepdims=True)) + eps_norm) * gain

def softmax_last(inputs):
    shifted = inputs - lax.optimization_barrier(jnp.max(inputs, axis=-1, keepdims=True))
    exponent = jnp.exp(shifted)
    return exponent / lax.optimization_barrier(jnp.sum(exponent, axis=-1, keepdims=True))

def attend(queries, key_rows, value_rows, bias_table, buckets):
    row_block = math.gcd(SEQ_LEN, 512)
    block_count = SEQ_LEN // row_block
    positions = jnp.arange(SEQ_LEN, dtype=jnp.int32)

    def one_block(item_index):
        sequence = item_index // block_count
        offset = item_index % block_count * row_block
        query_rows = lax.dynamic_slice_in_dim(queries[sequence], offset, row_block, 0)
        products = jnp.einsum('qhd,khd->hqk', query_rows, key_rows[sequence], precision=highest_score) * 0.125
        row_pos = offset + jnp.arange(row_block, dtype=jnp.int32)
        distance = row_pos[:, None] - positions[None, :]
        bucket_ids = buckets[jnp.maximum(distance, 0)]
        bias_tile = jnp.take(bias_table, bucket_ids, axis=0)
        scores = lowest_backward(products + jnp.transpose(bias_tile, (2, 0, 1)))
        scores = jnp.where((distance >= 0)[None], scores, masked_score)
        weights = lowest_pass(softmax_last(scores))
        return jnp.einsum('hqk,khd->qhd', weights, value_rows[sequence], precision=highest_score)
    attended = lax.map(jax.checkpoint(one_block), jnp.arange(SEQS * block_count, dtype=jnp.int32))
    return attended.reshape(SEQS, SEQ_LEN, HEADS * HEAD_DIM)

def route_slots(routes):
    blocks = SEQS * N_CTX
    route_pairs = routes.reshape(blocks, TOK_DEV * TOP)
    onehot = (route_pairs[:, :, None] == jnp.arange(EXPERTS, dtype=jnp.int32)[None, None, :]).astype(jnp.int32)
    earlier = jnp.cumsum(onehot, axis=1) - onehot
    slot_index = lax.optimization_barrier(jnp.sum(earlier * onehot, axis=-1))
    block_ids = jnp.arange(blocks, dtype=jnp.int32)[:, None]
    return (route_pairs * (blocks * CAP) + block_ids * CAP + slot_index).reshape(-1).astype(jnp.int32)

def run_experts(dispatched, w_in, w_out):

    def one_expert(operand):
        expert_rows, first_weight, second_weight = operand
        preact = lowest_backward(jnp.dot(expert_rows, first_weight, precision=highest_score))
        hidden = lowest_pass(jax.nn.gelu(preact, approximate=True))
        return lowest_backward(lowest_pass(jnp.dot(hidden, second_weight, precision=highest_score)))
    return lax.map(jax.checkpoint(one_expert), (dispatched, w_in, w_out))

def forward(tokens, w_query, w_key, w_value, attention_output_weight, router, norm1_gain, norm2_gain, attn_bias, w_in, w_out, routes, buckets):
    blocks = SEQS * N_CTX
    normed_input = lowest_pass(rms_scale(tokens, norm1_gain))

    def project(expert_weight):
        return lowest_backward(lowest_pass(jnp.einsum('ouf,fv->ouv', normed_input, expert_weight, precision=highest_score)))
    queries = project(w_query).reshape(SEQS, SEQ_LEN, HEADS, HEAD_DIM)
    key_rows = project(w_key).reshape(SEQS, SEQ_LEN, HEADS, HEAD_DIM)
    value_rows = project(w_value).reshape(SEQS, SEQ_LEN, HEADS, HEAD_DIM)
    context_rows = attend(queries, key_rows, value_rows, attn_bias, buckets)
    context_rows = lowest_backward(lowest_pass(context_rows))
    attention_result = lowest_backward(jnp.einsum('ouf,fv->ouv', context_rows, attention_output_weight, precision=highest_score))
    residual = tokens + attention_result
    second_choice = lowest_pass(rms_scale(residual, norm2_gain))
    router_logits = lowest_backward(jnp.einsum('ouf,fv->ouv', second_choice, router, precision=highest_score))
    chances = softmax_last(router_logits)
    picked = jnp.take_along_axis(chances, routes, axis=-1)
    gating = picked / lax.optimization_barrier(jnp.sum(picked, axis=-1, keepdims=True))
    destination = route_slots(routes)
    flattened = jnp.repeat(second_choice.reshape(-1, D), TOP, axis=0)
    dispatched = jnp.zeros((EXPERTS * blocks * CAP, D), jnp.float32).at[destination].set(flattened)
    dispatched = lowest_backward(dispatched)
    results = run_experts(dispatched.reshape(EXPERTS, blocks * CAP, D), w_in, w_out).reshape(-1, D)
    chosen = results[destination].reshape(SEQS, SEQ_LEN, TOP, D)
    mixture = lax.optimization_barrier(jnp.sum(gating[..., None] * chosen, axis=2))
    return residual + mixture

def reference(tokens, cotangent, w_query, w_key, w_value, attention_output_weight, router, norm1_gain, norm2_gain, attn_bias, w_in, w_out, routes, buckets):
    floats = (tokens, w_query, w_key, w_value, attention_output_weight, router, norm1_gain, norm2_gain, attn_bias, w_in, w_out)
    floats = tuple((item.astype(jnp.float32) for item in floats))

    def closed(*operands):
        return forward(*operands, routes.astype(jnp.int32), buckets.astype(jnp.int32))
    result, pullback = jax.vjp(closed, *floats)
    grads = pullback(cotangent.astype(jnp.float32))
    return (result.astype(jnp.bfloat16), grads[0], grads[1], grads[2], grads[3], grads[4], grads[5], grads[6], grads[7], grads[8], grads[9], grads[10])
```

```python
import functools

import jax
import jax.numpy as jnp
from jax import lax
from jax.experimental import pallas as pl
from jax.experimental.pallas import tpu as pltpu
from jax.sharding import PartitionSpec as P

bf16 = jnp.bfloat16
f32 = jnp.float32
eps_norm = 1e-06
masked_score = -1e30
vmem_bytes = 58 * 1024 * 1024


def dot_f32(a, b, contract):
    return lax.dot_general(a, b, (contract, ((), ())), preferred_element_type=f32)


def xor_move(value, axis, mask):
    count = lax.axis_size(axis)
    return lax.ppermute(value, axis, [(i, i ^ mask) for i in range(count)])


def shift_move(value, axis, step):
    count = lax.axis_size(axis)
    return lax.ppermute(value, axis, [(i, (i + step) % count) for i in range(count)])


def dp_offsets(count):
    offsets, mask = [0], count // 2
    while mask:
        offsets = offsets + [o ^ mask for o in offsets]
        mask //= 2
    return offsets


def gather_dp(block):
    count = lax.axis_size("dp")
    held, mask = [block], count // 2
    while mask:
        held = held + [xor_move(item, "dp", mask) for item in held]
        mask //= 2
    return held


def in_order(held, own):
    count = len(held)
    by_offset = [None] * count
    for offset, item in zip(dp_offsets(count), held):
        by_offset[offset] = item
    mask = 1
    while mask < count:
        swap = (own & mask) != 0
        by_offset = [jnp.where(swap, by_offset[o ^ mask], by_offset[o]) for o in range(count)]
        mask *= 2
    return by_offset


def scatter_sum_dp(parts):
    mask = 1
    while len(parts) > 1:
        half = len(parts) // 2
        arrived = [xor_move(item.astype(bf16), "dp", mask) for item in parts[half:]]
        parts = [mine + other.astype(f32) for mine, other in zip(parts[:half], arrived)]
        mask *= 2
    return parts[0]


def scatter_sum_dp_wide(parts):
    mask = 1
    while len(parts) > 1:
        half = len(parts) // 2
        arrived = [xor_move(item, "dp", mask) for item in parts[half:]]
        parts = [mine + other for mine, other in zip(parts[:half], arrived)]
        mask *= 2
    return parts[0]


def gather_ctx(blocks):
    half = lax.axis_size("ctx") // 2
    same = [blocks] + [[shift_move(item, "ctx", 2 * s) for item in blocks] for s in range(1, half)]
    across = [[xor_move(item, "ctx", 1) for item in entry] for entry in same]
    return same, across


def scatter_sum_ctx(same, across):
    half = lax.axis_size("ctx") // 2
    total = None
    order = list(range(1, half)) + [0]
    for s in order:
        arrived = xor_move(across[s].astype(bf16), "ctx", 1)
        joined = same[s].astype(f32) + arrived.astype(f32)
        if s:
            joined = shift_move(joined.astype(bf16), "ctx", -2 * s).astype(f32)
        total = joined if total is None else total + joined
    return total


def bias_kernel(vec_ref, tile_ref):
    heads, length = tile_ref.shape[0], tile_ref.shape[2]
    d = pl.program_id(0)
    start = pl.multiple_of(d * length, length)
    rows = lax.broadcasted_iota(jnp.int32, (8, 2 * length), 0)
    for h in range(heads):
        base = vec_ref[h : h + 1, pl.ds(start, 2 * length)]
        tile = jnp.broadcast_to(base, (8, 2 * length))
        for bit in (1, 2, 4):
            tile = jnp.where((rows & bit) != 0, pltpu.roll(tile, bit, 1), tile)
        size = 8
        while size < length:
            tile = jnp.concatenate([tile, pltpu.roll(tile, size, 1)], axis=0)
            size *= 2
        tile_ref[h, 0] = tile[:, length:].astype(bf16)


def bias_tiles(vec, heads, blocks, length):
    return pl.pallas_call(
        bias_kernel,
        grid=(blocks,),
        in_specs=[pl.BlockSpec(vec.shape, lambda d: (0, 0))],
        out_specs=pl.BlockSpec((heads, 1, length, length), lambda d: (0, d, 0, 0)),
        out_shape=jax.ShapeDtypeStruct((heads, blocks, length, length), bf16),
        compiler_params=pltpu.CompilerParams(vmem_limit_bytes=vmem_bytes),
        name="bias_tiles",
    )(vec)


def qkv_kernel(count, place_ref, gain_ref, weight_ref, *refs):
    token_refs, (normed_ref, out_ref) = refs[:count], refs[count:]
    length = token_refs[0].shape[0]
    third = weight_ref.shape[0] // 3
    for r in range(count):
        start = pl.multiple_of(place_ref[r] * length, length)
        x = token_refs[r][...].astype(f32)
        scale = lax.rsqrt(jnp.mean(x * x, axis=-1, keepdims=True) + eps_norm)
        normed = (x * scale * gain_ref[...]).astype(bf16)
        normed_ref[pl.ds(start, length), :] = normed
        made = dot_f32(weight_ref[...], normed, ((1,), (1,))).astype(bf16)
        out_ref[:third, pl.ds(start, length)] = (made[:third].astype(f32) * 0.125).astype(bf16)
        out_ref[third:, pl.ds(start, length)] = made[third:]


def project(tokens_held, places, gain, weight):
    count = len(tokens_held)
    length, width = tokens_held[0].shape
    vmem = pl.BlockSpec(memory_space=pltpu.VMEM)
    return pl.pallas_call(
        functools.partial(qkv_kernel, count),
        in_specs=[pl.BlockSpec(memory_space=pltpu.SMEM)] + [vmem] * (count + 2),
        out_specs=[vmem, vmem],
        out_shape=[
            jax.ShapeDtypeStruct((count * length, width), bf16),
            jax.ShapeDtypeStruct((weight.shape[0], count * length), bf16),
        ],
        compiler_params=pltpu.CompilerParams(vmem_limit_bytes=vmem_bytes),
        cost_estimate=pl.CostEstimate(
            flops=2 * count * length * width * weight.shape[0],
            bytes_accessed=2 * count * length * (2 * width + weight.shape[0]),
            transcendentals=0,
        ),
        name="project",
    )(places, gain, weight, *tokens_held)


def attend_kernel(heads, groups, splits, own_ref, qkv_ref, bias_ref, low_ref, wide_ref, lse_ref, k3, acc):
    length = bias_ref.shape[2]
    blocks = bias_ref.shape[1]
    dim = k3.shape[2]
    third = heads * dim
    for h in range(heads):

        def turn(c, _):
            start = pl.multiple_of(c * length, length)
            k3[h, pl.ds(start, length), :] = qkv_ref[
                third + h * dim : third + (h + 1) * dim, pl.ds(start, length)
            ].T
            return 0

        lax.fori_loop(0, blocks, turn, 0)
    own = own_ref[0]
    for j in range(groups):
        block = j * splits + own
        q_start = pl.multiple_of(block * length, length)
        acc[...] = jnp.zeros_like(acc)

        def visit(c, state):
            start = pl.multiple_of(c * length, length)
            out = []
            for h in range(heads):
                top, total = state[h]
                q = qkv_ref[h * dim : (h + 1) * dim, pl.ds(q_start, length)]
                s = dot_f32(k3[h, pl.ds(start, length), :], q, ((1,), (0,)))
                s = s + bias_ref[h, block - c].astype(f32)
                new_top = jnp.maximum(top, jnp.max(s, axis=0, keepdims=True))
                p = jnp.exp(s - new_top)
                fade = jnp.exp(top - new_top)
                total = total * fade + jnp.sum(p, axis=0, keepdims=True)
                v = qkv_ref[2 * third + h * dim : 2 * third + (h + 1) * dim, pl.ds(start, length)]
                acc[h] = acc[h] * fade + dot_f32(v, p.astype(bf16), ((1,), (0,)))
                out.append((new_top, total))
            return tuple(out)

        begin = tuple(
            (jnp.full((1, length), masked_score, f32), jnp.zeros((1, length), f32)) for _ in range(heads)
        )
        state = lax.fori_loop(0, block + 1, visit, begin)
        for h in range(heads):
            top, total = state[h]
            context = acc[h] / total
            wide_ref[j, h * dim : (h + 1) * dim, :] = context
            low_ref[j, h * dim : (h + 1) * dim, :] = context.astype(bf16)
            lse_ref[j, h : h + 1, :] = top + jnp.log(total)


def attend(own, qkv, tiles, groups, splits):
    heads, blocks, length, _ = tiles.shape
    third = qkv.shape[0] // 3
    dim = third // heads
    vmem = pl.BlockSpec(memory_space=pltpu.VMEM)
    units = heads * groups * (blocks + 1) // 2
    return pl.pallas_call(
        functools.partial(attend_kernel, heads, groups, splits),
        in_specs=[pl.BlockSpec(memory_space=pltpu.SMEM), vmem, vmem],
        out_specs=[vmem] * 3,
        out_shape=[
            jax.ShapeDtypeStruct((groups, third, length), bf16),
            jax.ShapeDtypeStruct((groups, third, length), f32),
            jax.ShapeDtypeStruct((groups, 8, length), f32),
        ],
        scratch_shapes=[pltpu.VMEM((heads, blocks * length, dim), bf16), pltpu.VMEM((heads, dim, length), f32)],
        compiler_params=pltpu.CompilerParams(vmem_limit_bytes=vmem_bytes),
        cost_estimate=pl.CostEstimate(
            flops=units * length * length * 256 * 4,
            bytes_accessed=10 * 1024 * 1024,
            transcendentals=units * length * length,
        ),
        name="attend",
    )(own, qkv, tiles)


def attend_back_kernel(
    heads, groups, splits, own_ref, qkv_ref, bias_ref, grad_ref, wide_ref, lse_ref,
    out_ref, diag_ref, k3, v3, grad_k, grad_v, grad_q, grad_b,
):
    length = bias_ref.shape[2]
    blocks = bias_ref.shape[1]
    dim = k3.shape[2]
    third = heads * dim
    for h in range(heads):

        def turn(c, _):
            start = pl.multiple_of(c * length, length)
            k3[h, pl.ds(start, length), :] = qkv_ref[
                third + h * dim : third + (h + 1) * dim, pl.ds(start, length)
            ].T
            v3[h, pl.ds(start, length), :] = qkv_ref[
                2 * third + h * dim : 2 * third + (h + 1) * dim, pl.ds(start, length)
            ].T
            grad_b[h, c] = jnp.zeros((length, length), f32)
            return 0

        lax.fori_loop(0, blocks, turn, 0)
    grad_k[...] = jnp.zeros_like(grad_k)
    grad_v[...] = jnp.zeros_like(grad_v)
    out_ref[:third, :] = jnp.zeros((third, blocks * length), bf16)
    own = own_ref[0]
    for j in range(groups):
        block = j * splits + own
        q_start = pl.multiple_of(block * length, length)
        grad_q[...] = jnp.zeros_like(grad_q)
        delta = []
        for h in range(heads):
            rows = slice(h * dim, (h + 1) * dim)
            delta.append(
                jnp.sum(grad_ref[j, rows, :].astype(f32) * wide_ref[j, rows, :], axis=0, keepdims=True)
            )

        def visit(c, state):
            start = pl.multiple_of(c * length, length)
            for h in range(heads):
                rows = slice(h * dim, (h + 1) * dim)
                q = qkv_ref[h * dim : (h + 1) * dim, pl.ds(q_start, length)]
                g = grad_ref[j, rows, :]
                s = dot_f32(k3[h, pl.ds(start, length), :], q, ((1,), (0,)))
                s = s + bias_ref[h, block - c].astype(f32)
                p = jnp.exp(s - lse_ref[j, h : h + 1, :])
                dp = dot_f32(v3[h, pl.ds(start, length), :], g, ((1,), (0,)))
                ds = (p * (dp - state[h])).astype(bf16)
                grad_v[rows, pl.ds(start, length)] += dot_f32(g, p.astype(bf16), ((1,), (1,)))
                grad_k[rows, pl.ds(start, length)] += dot_f32(q, ds, ((1,), (1,)))
                kt = qkv_ref[third + h * dim : third + (h + 1) * dim, pl.ds(start, length)]
                grad_q[rows, :] += dot_f32(kt, ds, ((1,), (0,)))
                grad_b[h, block - c] += ds.astype(f32)
            return state

        lax.fori_loop(0, block + 1, visit, tuple(delta))
        out_ref[:third, pl.ds(q_start, length)] = (grad_q[...] * 0.125).astype(bf16)
    out_ref[third : 2 * third, :] = grad_k[...].astype(bf16)
    out_ref[2 * third :, :] = grad_v[...].astype(bf16)
    row = lax.broadcasted_iota(jnp.int32, (8, 2 * length), 0)

    def diagonals(d, _):
        for h in range(heads):
            tile = grad_b[h, d]
            tile = jnp.concatenate([jnp.zeros_like(tile), tile], axis=1)
            size = length // 2
            while size >= 8:
                tile = tile[:size] + pltpu.roll(tile[size:], 2 * length - size, 1)
                size //= 2
            for bit in (1, 2, 4):
                tile = jnp.where((row & bit) != 0, pltpu.roll(tile, 2 * length - bit, 1), tile)
            diag_ref[d, h : h + 1, :] = jnp.sum(tile, axis=0, keepdims=True)
        return 0

    lax.fori_loop(0, blocks, diagonals, 0)


def attend_back(own, qkv, tiles, grad_context, wide, lse, groups, splits):
    heads, blocks, length, _ = tiles.shape
    third = qkv.shape[0] // 3
    dim = third // heads
    vmem = pl.BlockSpec(memory_space=pltpu.VMEM)
    units = heads * groups * (blocks + 1) // 2
    return pl.pallas_call(
        functools.partial(attend_back_kernel, heads, groups, splits),
        in_specs=[pl.BlockSpec(memory_space=pltpu.SMEM)] + [vmem] * 5,
        out_specs=[vmem] * 2,
        out_shape=[
            jax.ShapeDtypeStruct((3 * third, blocks * length), bf16),
            jax.ShapeDtypeStruct((blocks, 8, 2 * length), f32),
        ],
        scratch_shapes=[
            pltpu.VMEM((heads, blocks * length, dim), bf16),
            pltpu.VMEM((heads, blocks * length, dim), bf16),
            pltpu.VMEM((third, blocks * length), f32),
            pltpu.VMEM((third, blocks * length), f32),
            pltpu.VMEM((third, length), f32),
            pltpu.VMEM((heads, blocks, length, length), f32),
        ],
        compiler_params=pltpu.CompilerParams(vmem_limit_bytes=vmem_bytes),
        cost_estimate=pl.CostEstimate(
            flops=units * length * length * 256 * 10,
            bytes_accessed=20 * 1024 * 1024,
            transcendentals=units * length * length,
        ),
        name="attend_back",
    )(own, qkv, tiles, grad_context, wide, lse)


def expert_kernel(x_ref, g_ref, weight_ref, out_ref, gx_ref, grad_ref, sum_rows, sum_gx, sum_grad):
    step = pl.program_id(0)
    rows = x_ref.shape[0]
    units = weight_ref.shape[1] // 2
    tile = min(rows, 512)
    root = 0.7978845608028654

    @pl.when(step == 0)
    def _():
        sum_rows[...] = jnp.zeros_like(sum_rows)
        sum_gx[...] = jnp.zeros_like(sum_gx)

    first = weight_ref[0, :units, :]
    second = weight_ref[0, units:, :]
    for at in range(0, rows, tile):
        part = slice(at, at + tile)
        x = x_ref[part, :]
        g = g_ref[part, :]
        pre = dot_f32(x, first, ((1,), (1,)))
        back = dot_f32(g, second, ((1,), (1,)))
        square = pre * pre
        bent = jnp.tanh(root * (pre + 0.044715 * pre * square))
        half = 0.5 * (1.0 + bent)
        hidden = (pre * half).astype(bf16)
        slope = half + 0.5 * pre * (1.0 - bent * bent) * (root * (1.0 + 0.134145 * square))
        gp = (back * slope).astype(bf16)
        sum_rows[part, :] += dot_f32(hidden, second, ((1,), (0,)))
        sum_gx[part, :] += dot_f32(gp, first, ((1,), (0,)))
        grad_first = dot_f32(gp, x, ((0,), (0,)))
        grad_second = dot_f32(hidden, g, ((0,), (0,)))
        if at == 0:
            sum_grad[:units, :] = grad_first
            sum_grad[units:, :] = grad_second
        else:
            sum_grad[:units, :] += grad_first
            sum_grad[units:, :] += grad_second
    grad_ref[0] = sum_grad[...].astype(bf16)

    @pl.when(step == pl.num_programs(0) - 1)
    def _():
        out_ref[...] = sum_rows[...].astype(bf16)
        gx_ref[...] = sum_gx[...].astype(bf16)


def run_expert(x, g, weights):
    rows, width = x.shape
    shards, units = weights.shape[0], weights.shape[1] // 2
    row_spec = pl.BlockSpec((rows, width), lambda i: (0, 0))
    shard_spec = pl.BlockSpec((1, 2 * units, width), lambda i: (i, 0, 0))
    return pl.pallas_call(
        expert_kernel,
        grid=(shards,),
        in_specs=[row_spec, row_spec, shard_spec],
        out_specs=[row_spec, row_spec, shard_spec],
        out_shape=[jax.ShapeDtypeStruct((rows, width), bf16)] * 2 + [jax.ShapeDtypeStruct(weights.shape, bf16)],
        scratch_shapes=[pltpu.VMEM((rows, width), f32)] * 2 + [pltpu.VMEM((2 * units, width), f32)],
        compiler_params=pltpu.CompilerParams(vmem_limit_bytes=vmem_bytes),
        cost_estimate=pl.CostEstimate(
            flops=12 * rows * width * units * shards,
            bytes_accessed=8 * rows * width + 8 * shards * width * units,
            transcendentals=rows * units * shards,
        ),
        name="run_expert",
    )(x, g, weights)


def norm_back(x, gain, grad):
    scale = lax.rsqrt(jnp.mean(x * x, axis=-1, keepdims=True) + eps_norm)
    weighted = grad * gain
    inner = jnp.mean(weighted * x, axis=-1, keepdims=True)
    return scale * weighted - x * (scale * scale * scale) * inner, jnp.sum(grad * x * scale, axis=0)


def body(
    tokens, cotangent, w_query, w_key, w_value, attention_output_weight, router, norm1_gain, norm2_gain,
    attn_bias, w_in, w_out, routes, buckets,
):
    n_ctx = lax.axis_size("ctx")
    n_dp = lax.axis_size("dp")
    ctx_at = lax.axis_index("ctx")
    dp_at = lax.axis_index("dp")
    half = n_ctx // 2
    _, length, width = tokens.shape
    all_heads = attn_bias.shape[1]
    bucket_count = attn_bias.shape[0] * n_dp
    experts = router.shape[1]
    groups = 4
    splits = n_ctx // groups
    heads = all_heads // groups
    dim = width // all_heads
    third = heads * dim
    group_at = ctx_at // splits
    split_at = ctx_at % splits
    rows_dp = w_query.shape[0]

    bias_flat = attn_bias.reshape(1, -1)
    small = jnp.concatenate(
        [
            router.T,
            norm1_gain[None],
            norm2_gain[None],
            jnp.pad(bias_flat, ((0, 0), (0, 2 * rows_dp - bias_flat.shape[1]))).reshape(2, rows_dp)
            if bias_flat.shape[1] > rows_dp
            else jnp.pad(bias_flat, ((0, 0), (0, rows_dp - bias_flat.shape[1]))),
        ],
        axis=0,
    )
    small_all = jnp.stack(in_order(gather_dp(small), dp_at))
    router_weight = small_all[:, :experts, :].transpose(1, 0, 2).reshape(experts, width)
    gain_first = small_all[:, experts, :].reshape(1, width).astype(f32)
    gain_second = small_all[:, experts + 1, :].reshape(1, width).astype(f32)
    bias_table = (
        small_all[:, experts + 2 :, :].reshape(n_dp, -1)[:, : bias_flat.shape[1]].reshape(bucket_count, all_heads)
    )

    own_columns = [
        lax.dynamic_slice_in_dim(w, group_at * third, third, axis=1).T for w in (w_query, w_key, w_value)
    ]
    qkv_part = jnp.concatenate(own_columns, axis=0)
    tok_same, tok_across = gather_ctx([tokens[0]])
    tokens_held = [entry[0] for entry in tok_same + tok_across]
    qkv_weight = jnp.concatenate(in_order(gather_dp(qkv_part), dp_at), axis=1)
    output_weight = jnp.concatenate(in_order(gather_dp(attention_output_weight), dp_at), axis=0)
    upstream_rows = jnp.concatenate(gather_dp(cotangent[0]), axis=0)
    routes_rows = jnp.concatenate(gather_dp(routes[0]), axis=0)

    units = w_in.shape[2]
    expert_weights = lax.all_gather(jnp.concatenate([w_in[0].T, w_out[0]], axis=0), "ctx", axis=0)

    onehot = (buckets[:, None] == jnp.arange(bucket_count, dtype=jnp.int32)[None, :]).astype(bf16)
    bias_own = lax.dynamic_slice_in_dim(bias_table, group_at * heads, heads, axis=1)
    per_distance = dot_f32(bias_own, onehot, ((0,), (1,)))
    vec = jnp.concatenate([jnp.full((heads, length), masked_score, f32), per_distance], axis=1)
    vec = jnp.pad(vec, ((0, 8 - heads), (0, 0)))
    tiles = bias_tiles(vec, heads, n_ctx, length)

    z_at, x_at = ctx_at // 2, ctx_at % 2
    places = jnp.stack(
        [((z_at - s) % half) * 2 + x_at for s in range(half)]
        + [((z_at - s) % half) * 2 + (1 - x_at) for s in range(half)]
    ).astype(jnp.int32)
    normed, qkv = project(tokens_held, places, gain_first, qkv_weight)
    own_split = split_at.astype(jnp.int32).reshape(1)
    low, wide, lse = attend(own_split, qkv, tiles, groups, splits)
    index_groups = [[g * splits + b for g in range(groups)] for b in range(splits)]
    context_t = lax.all_to_all(
        low, "ctx", split_axis=0, concat_axis=0, tiled=True, axis_index_groups=index_groups
    ).reshape(width, length)

    resid_in = tokens[0].astype(f32)
    residual = resid_in + dot_f32(context_t, output_weight, ((0,), (0,)))
    scale2 = lax.rsqrt(jnp.mean(residual * residual, axis=-1, keepdims=True) + eps_norm)
    second = (residual * scale2 * gain_second).astype(bf16)
    second_rows = jnp.concatenate(gather_dp(second), axis=0)

    def gate(rows, pairs):
        logits = dot_f32(rows, router_weight, ((1,), (1,)))
        shifted = jnp.exp(logits - jnp.max(logits, axis=-1, keepdims=True))
        chances = shifted / jnp.sum(shifted, axis=-1, keepdims=True)
        named = jnp.arange(experts, dtype=jnp.int32)[None, :]
        select = jnp.zeros(chances.shape, f32)
        for k in range(pairs.shape[1]):
            select = select + (pairs[:, k : k + 1] == named).astype(f32)
        total = jnp.sum(select * chances, axis=-1, keepdims=True)
        return chances, select, total

    chances_r, select_r, total_r = gate(second_rows, routes_rows)
    own_expert = (jnp.arange(experts, dtype=jnp.int32)[None, :] == dp_at).astype(f32)
    gate_own = jnp.sum(own_expert * select_r * chances_r / total_r, axis=-1, keepdims=True)
    upstream_f = upstream_rows.astype(f32)
    grad_rows = (gate_own * upstream_f).astype(bf16)

    chunk = min(n_dp * length, 1024)
    made = [
        run_expert(second_rows[at : at + chunk], grad_rows[at : at + chunk], expert_weights)
        for at in range(0, n_dp * length, chunk)
    ]
    expert_result = jnp.concatenate([m[0] for m in made], axis=0).astype(f32)
    grad_dispatched = jnp.concatenate([m[1] for m in made], axis=0).astype(f32)
    grad_expert = made[0][2]
    if len(made) > 1:
        grad_expert = sum(m[2].astype(f32) for m in made).astype(bf16)
    grad_expert = lax.psum_scatter(grad_expert, "ctx", scatter_dimension=0, tiled=False).astype(f32)
    grad_w_in = grad_expert[:units].T[None]
    grad_w_out = grad_expert[units:][None]
    grad_gate_rows = jnp.sum(upstream_f * expert_result, axis=-1, keepdims=True) * (own_expert * select_r)
    mixed = gate_own * expert_result
    routed = jnp.sum(own_expert * select_r, axis=-1, keepdims=True)
    grad_dispatched = grad_dispatched * routed

    def by_device(rows):
        return [rows[k * length : (k + 1) * length] for k in range(n_dp)]

    moe_grad = scatter_sum_dp(by_device(grad_dispatched))
    grad_gating = scatter_sum_dp_wide(by_device(grad_gate_rows))

    chances, select, total = gate(second, routes[0])
    inner = jnp.sum(select * grad_gating * chances, axis=-1, keepdims=True)
    grad_chances = select * (grad_gating / total - inner / (total * total))
    grad_logits = (chances * (grad_chances - jnp.sum(chances * grad_chances, axis=-1, keepdims=True))).astype(bf16)
    grad_router = dot_f32(grad_logits, second, ((0,), (0,)))
    grad_second = moe_grad + dot_f32(grad_logits, router_weight, ((1,), (0,)))
    grad_norm, grad_gain_second = norm_back(residual, gain_second, grad_second)
    grad_residual = cotangent[0].astype(f32) + grad_norm
    grad_attn = grad_residual.astype(bf16)

    mixed, _ = lax.optimization_barrier((mixed, grad_attn))
    mixture = scatter_sum_dp(by_device(mixed))
    layer_out = (residual + mixture).astype(bf16)[None]

    grad_context_t = dot_f32(output_weight, grad_attn, ((1,), (1,))).astype(bf16)
    grad_context = lax.all_to_all(
        grad_context_t.reshape(groups, third, length),
        "ctx", split_axis=0, concat_axis=0, tiled=True, axis_index_groups=index_groups,
    )
    grad_output_w = dot_f32(context_t, grad_attn, ((1,), (0,))).astype(bf16)
    grad_output_w = lax.all_to_all(
        grad_output_w.reshape(n_dp, rows_dp, width), "dp", split_axis=0, concat_axis=0, tiled=True
    )
    grad_output_w = jnp.sum(grad_output_w.astype(f32), axis=0)
    grad_output_w = grad_output_w + xor_move(grad_output_w.astype(bf16), "ctx", 1).astype(f32)
    pieces = grad_output_w.astype(bf16)
    for s in range(1, half):
        grad_output_w = grad_output_w + shift_move(pieces, "ctx", 2 * s).astype(f32)
    grad_qkv, diag = attend_back(own_split, qkv, tiles, grad_context, wide, lse, groups, splits)

    gw = dot_f32(grad_qkv, normed, ((1,), (0,)))
    grad_gain_first = jnp.sum(gw * qkv_weight.astype(f32), axis=0) / gain_first[0]
    by_distance = diag[:, :heads, length:].transpose(1, 0, 2).reshape(heads, -1)
    nearer = diag[1:, :heads, :length].transpose(1, 0, 2).reshape(heads, -1)
    by_distance = by_distance + jnp.pad(nearer, ((0, 0), (0, length)))
    grad_bias = lax.dot_general(
        onehot.astype(f32), by_distance, (((0,), (1,)), ((), ())), precision=lax.Precision.HIGHEST
    )
    in_group = (jnp.arange(groups) == group_at).astype(f32)
    grad_bias = (in_group[None, :, None] * grad_bias[:, None, :]).reshape(n_dp, -1)
    bias_rows = -(-grad_bias.shape[1] // rows_dp)
    grad_bias = jnp.pad(grad_bias, ((0, 0), (0, bias_rows * rows_dp - grad_bias.shape[1])))
    small_count = experts + 2 + bias_rows
    parts = jnp.concatenate(
        [
            gw.reshape(3 * third, n_dp, rows_dp).transpose(1, 0, 2),
            grad_router.reshape(experts, n_dp, rows_dp).transpose(1, 0, 2),
            grad_gain_first.reshape(n_dp, 1, rows_dp),
            grad_gain_second.reshape(n_dp, 1, rows_dp),
            grad_bias.reshape(n_dp, bias_rows, rows_dp),
            jnp.zeros((n_dp, -small_count % 16, rows_dp), f32),
        ],
        axis=1,
    ).astype(bf16)
    parts = lax.all_to_all(parts, "dp", split_axis=0, concat_axis=0, tiled=True)
    gw = jnp.sum(parts.astype(f32), axis=0)
    mask = 1
    while mask < splits:
        gw = gw + xor_move(gw.astype(bf16), "ctx", mask).astype(f32)
        mask *= 2
    gw = gw.astype(bf16)
    held = [gw] + [shift_move(gw, "ctx", -splits * s) for s in range(1, groups)]
    small_grads = sum(entry[3 * third :].astype(f32) for entry in held)
    dense = [entry[: 3 * third] for entry in held]
    twice = jnp.concatenate(dense + dense, axis=0)
    begin = ((groups - group_at) % groups) * (3 * third)
    ordered = lax.dynamic_slice_in_dim(twice, begin, groups * 3 * third, axis=0)
    ordered = ordered.reshape(groups, 3, third, rows_dp).transpose(1, 3, 0, 2).reshape(3, rows_dp, width).astype(f32)
    grad_router = small_grads[:experts].T
    grad_gain_first = small_grads[experts]
    grad_gain_second = small_grads[experts + 1]
    grad_bias = small_grads[experts + 2 : small_count].reshape(-1)[: bias_flat.shape[1]].reshape(attn_bias.shape)

    partial = dot_f32(grad_qkv, qkv_weight, ((0,), (0,))).astype(bf16)

    def block_of(s, across):
        at = ((z_at - s) % half) * 2 + (1 - x_at if across else x_at)
        return lax.dynamic_slice_in_dim(partial, at * length, length, axis=0)

    grad_normed = scatter_sum_ctx(
        [block_of(s, False) for s in range(half)], [block_of(s, True) for s in range(half)]
    )
    grad_in_norm = norm_back(resid_in, gain_first, grad_normed)[0]
    input_grad = (grad_residual + grad_in_norm)[None]
    return (
        layer_out, input_grad, ordered[0], ordered[1], ordered[2], grad_output_w, grad_router,
        grad_gain_first, grad_gain_second, grad_bias, grad_w_in, grad_w_out,
    )


def solution(mesh):
    in_specs = (
        P("dp", "ctx", None),
        P("dp", "ctx", None),
        P("dp", None),
        P("dp", None),
        P("dp", None),
        P("dp", None),
        P("dp", None),
        P("dp"),
        P("dp"),
        P("dp", None),
        P("dp", None, "ctx"),
        P("dp", "ctx", None),
        P("dp", "ctx", None),
        P(),
    )
    out_specs = (
        P("dp", "ctx", None),
        P("dp", "ctx", None),
        P("dp", None),
        P("dp", None),
        P("dp", None),
        P("dp", None),
        P("dp", None),
        P("dp"),
        P("dp"),
        P("dp", None),
        P("dp", None, "ctx"),
        P("dp", "ctx", None),
    )
    return jax.shard_map(body, mesh=mesh, in_specs=in_specs, out_specs=out_specs, check_vma=False)
```

```python
import functools

import jax
import jax.numpy as jnp
from jax import lax
from jax.experimental import pallas as pl
from jax.experimental.pallas import tpu as pltpu
from jax.sharding import PartitionSpec as P

bf16 = jnp.bfloat16
f32 = jnp.float32
eps_norm = 1e-06
masked_score = -1e30
vmem_bytes = 58 * 1024 * 1024


def dot_f32(a, b, contract):
    return lax.dot_general(a, b, (contract, ((), ())), preferred_element_type=f32)


def xor_move(value, axis, mask):
    count = lax.axis_size(axis)
    return lax.ppermute(value, axis, [(i, i ^ mask) for i in range(count)])


def shift_move(value, axis, step):
    count = lax.axis_size(axis)
    return lax.ppermute(value, axis, [(i, (i + step) % count) for i in range(count)])


def dp_offsets(count):
    offsets, mask = [0], count // 2
    while mask:
        offsets = offsets + [o ^ mask for o in offsets]
        mask //= 2
    return offsets


def gather_dp(block, after):
    count = lax.axis_size("dp")
    held, mask = [block], count // 2
    while mask:
        if mask == 1:
            held, _ = lax.optimization_barrier((held, after))
        held = held + [xor_move(item, "dp", mask) for item in held]
        mask //= 2
    return held


def in_order(held, own):
    count = len(held)
    by_offset = [None] * count
    for offset, item in zip(dp_offsets(count), held):
        by_offset[offset] = item
    mask = 1
    while mask < count:
        swap = (own & mask) != 0
        by_offset = [jnp.where(swap, by_offset[o ^ mask], by_offset[o]) for o in range(count)]
        mask *= 2
    return by_offset


def gather_rows(block):
    far = lax.axis_size("dp") // 2
    items = [block, xor_move(block, "ctx", 1)]
    items = items + [xor_move(item, "dp", far) for item in items]
    rows = jnp.concatenate(items, axis=0)
    mask = far // 2
    while mask > 1:
        rows = jnp.concatenate([rows, xor_move(rows, "dp", mask)], axis=0)
        mask //= 2
    return rows, xor_move(rows, "dp", 1)


def scatter_sum_rows(near, other, sent):
    far = lax.axis_size("dp") // 2
    rows = near.astype(f32) + xor_move(other.astype(sent), "dp", 1).astype(f32)
    rows = rows.astype(sent) if far > 2 else rows
    mask = 2
    while mask < far:
        cut = rows.shape[0] // 2
        arrived = xor_move(rows[cut:].astype(sent), "dp", mask)
        rows = (rows[:cut].astype(f32) + arrived.astype(f32)).astype(sent)
        mask *= 2
    cut = rows.shape[0] // 4
    own, over_x, over_y, over_both = [rows[k * cut : (k + 1) * cut] for k in range(4)]
    arrived = xor_move(over_both.astype(sent), "dp", far)
    over_x = (over_x.astype(f32) + arrived.astype(f32)).astype(sent)
    own = own.astype(f32) + xor_move(over_y.astype(sent), "dp", far).astype(f32)
    return own, over_x


def scatter_sum_end(own, over_x):
    return own + xor_move(over_x, "ctx", 1).astype(f32)


def gather_ctx(blocks):
    half = lax.axis_size("ctx") // 2
    same = [blocks] + [[shift_move(item, "ctx", 2 * s) for item in blocks] for s in range(1, half)]
    across = [[xor_move(item, "ctx", 1) for item in entry] for entry in same]
    return same, across


def bias_kernel(vec_ref, tile_ref):
    heads, length = tile_ref.shape[0], tile_ref.shape[2]
    d = pl.program_id(0)
    start = pl.multiple_of(d * length, length)
    rows = lax.broadcasted_iota(jnp.int32, (8, 2 * length), 0)
    for h in range(heads):
        base = vec_ref[h : h + 1, pl.ds(start, 2 * length)]
        tile = jnp.broadcast_to(base, (8, 2 * length))
        for bit in (1, 2, 4):
            tile = jnp.where((rows & bit) != 0, pltpu.roll(tile, bit, 1), tile)
        size = 8
        while size < length:
            tile = jnp.concatenate([tile, pltpu.roll(tile, size, 1)], axis=0)
            size *= 2
        tile_ref[h, 0] = tile[:, length:].astype(bf16)


def bias_tiles(vec, heads, blocks, length):
    return pl.pallas_call(
        bias_kernel,
        grid=(blocks,),
        in_specs=[pl.BlockSpec(vec.shape, lambda d: (0, 0))],
        out_specs=pl.BlockSpec((heads, 1, length, length), lambda d: (0, d, 0, 0)),
        out_shape=jax.ShapeDtypeStruct((heads, blocks, length, length), bf16),
        compiler_params=pltpu.CompilerParams(vmem_limit_bytes=vmem_bytes),
        name="bias_tiles",
    )(vec)


def qkv_kernel(count, place_ref, gain_ref, weight_ref, *refs):
    token_refs, (normed_ref, out_ref) = refs[:count], refs[count:]
    length = token_refs[0].shape[0]
    third = weight_ref.shape[0] // 3
    for r in range(count):
        place = place_ref[r]
        start = pl.multiple_of(place * length, length)
        x = token_refs[r][...].astype(f32)
        scale = lax.rsqrt(jnp.mean(x * x, axis=-1, keepdims=True) + eps_norm)
        normed = (x * scale * gain_ref[...]).astype(bf16)
        normed_ref[place] = normed
        made = dot_f32(weight_ref[...], normed, ((1,), (1,))).astype(bf16)
        out_ref[:third, pl.ds(start, length)] = (made[:third].astype(f32) * 0.125).astype(bf16)
        out_ref[third:, pl.ds(start, length)] = made[third:]


def project(tokens_held, places, gain, weight):
    count = len(tokens_held)
    length, width = tokens_held[0].shape
    vmem = pl.BlockSpec(memory_space=pltpu.VMEM)
    return pl.pallas_call(
        functools.partial(qkv_kernel, count),
        in_specs=[pl.BlockSpec(memory_space=pltpu.SMEM)] + [vmem] * (count + 2),
        out_specs=[vmem, vmem],
        out_shape=[
            jax.ShapeDtypeStruct((count, length, width), bf16),
            jax.ShapeDtypeStruct((weight.shape[0], count * length), bf16),
        ],
        compiler_params=pltpu.CompilerParams(vmem_limit_bytes=vmem_bytes),
        cost_estimate=pl.CostEstimate(
            flops=2 * count * length * width * weight.shape[0],
            bytes_accessed=2 * count * length * (2 * width + weight.shape[0]),
            transcendentals=0,
        ),
        name="project",
    )(places, gain, weight, *tokens_held)


def attend_kernel(heads, groups, splits, own_ref, qkv_ref, bias_ref, low_ref, wide_ref, lse_ref, k3, acc):
    length = bias_ref.shape[2]
    blocks = bias_ref.shape[1]
    dim = k3.shape[2]
    third = heads * dim
    for h in range(heads):

        def turn(c, _):
            start = pl.multiple_of(c * length, length)
            k3[h, pl.ds(start, length), :] = qkv_ref[
                third + h * dim : third + (h + 1) * dim, pl.ds(start, length)
            ].T
            return 0

        lax.fori_loop(0, blocks, turn, 0)
    own = own_ref[0]
    for j in range(groups):
        block = j * splits + own
        q_start = pl.multiple_of(block * length, length)
        acc[...] = jnp.zeros_like(acc)

        def visit(c, state):
            start = pl.multiple_of(c * length, length)
            out = []
            for h in range(heads):
                top, total = state[h]
                q = qkv_ref[h * dim : (h + 1) * dim, pl.ds(q_start, length)]
                s = dot_f32(k3[h, pl.ds(start, length), :], q, ((1,), (0,)))
                s = s + bias_ref[h, block - c].astype(f32)
                new_top = jnp.maximum(top, jnp.max(s, axis=0, keepdims=True))
                p = jnp.exp(s - new_top)
                fade = jnp.exp(top - new_top)
                total = total * fade + jnp.sum(p, axis=0, keepdims=True)
                v = qkv_ref[2 * third + h * dim : 2 * third + (h + 1) * dim, pl.ds(start, length)]
                acc[h] = acc[h] * fade + dot_f32(v, p.astype(bf16), ((1,), (0,)))
                out.append((new_top, total))
            return tuple(out)

        begin = tuple(
            (jnp.full((1, length), masked_score, f32), jnp.zeros((1, length), f32)) for _ in range(heads)
        )
        state = lax.fori_loop(0, block + 1, visit, begin)
        for h in range(heads):
            top, total = state[h]
            context = acc[h] / total
            wide_ref[j, h * dim : (h + 1) * dim, :] = context
            low_ref[j, h * dim : (h + 1) * dim, :] = context.astype(bf16)
            lse_ref[j, h : h + 1, :] = top + jnp.log(total)


def attend(own, qkv, tiles, groups, splits):
    heads, blocks, length, _ = tiles.shape
    third = qkv.shape[0] // 3
    dim = third // heads
    vmem = pl.BlockSpec(memory_space=pltpu.VMEM)
    units = heads * groups * (blocks + 1) // 2
    return pl.pallas_call(
        functools.partial(attend_kernel, heads, groups, splits),
        in_specs=[pl.BlockSpec(memory_space=pltpu.SMEM), vmem, vmem],
        out_specs=[vmem] * 3,
        out_shape=[
            jax.ShapeDtypeStruct((groups, third, length), bf16),
            jax.ShapeDtypeStruct((groups, third, length), f32),
            jax.ShapeDtypeStruct((groups, 8, length), f32),
        ],
        scratch_shapes=[pltpu.VMEM((heads, blocks * length, dim), bf16), pltpu.VMEM((heads, dim, length), f32)],
        compiler_params=pltpu.CompilerParams(vmem_limit_bytes=vmem_bytes),
        cost_estimate=pl.CostEstimate(
            flops=units * length * length * 256 * 4,
            bytes_accessed=10 * 1024 * 1024,
            transcendentals=units * length * length,
        ),
        name="attend",
    )(own, qkv, tiles)


def attend_back_kernel(
    heads, groups, splits, own_ref, qkv_ref, bias_ref, grad_ref, wide_ref, lse_ref, normed_ref, weight_ref,
    gain_ref, named_ref, small_ref, q_ref, *refs,
):
    kv_refs, parts_ref = refs[:splits], refs[splits]
    diag_ref, sum_w, k3, v3, grad_k, grad_v, grad_q, grad_b = refs[splits + 1 :]
    length = bias_ref.shape[2]
    blocks = bias_ref.shape[1]
    dim = k3.shape[2]
    third = heads * dim
    for h in range(heads):

        def turn(c, _):
            start = pl.multiple_of(c * length, length)
            k3[h, pl.ds(start, length), :] = qkv_ref[
                third + h * dim : third + (h + 1) * dim, pl.ds(start, length)
            ].T
            v3[h, pl.ds(start, length), :] = qkv_ref[
                2 * third + h * dim : 2 * third + (h + 1) * dim, pl.ds(start, length)
            ].T
            grad_b[h, c] = jnp.zeros((length, length), f32)
            return 0

        lax.fori_loop(0, blocks, turn, 0)
    sum_w[...] = jnp.zeros_like(sum_w)
    grad_k[...] = jnp.zeros_like(grad_k)
    grad_v[...] = jnp.zeros_like(grad_v)
    own = own_ref[0]
    for j in range(groups):
        block = j * splits + own
        q_start = pl.multiple_of(block * length, length)
        grad_q[...] = jnp.zeros_like(grad_q)
        delta = []
        for h in range(heads):
            rows = slice(h * dim, (h + 1) * dim)
            delta.append(
                jnp.sum(grad_ref[j, rows, :].astype(f32) * wide_ref[j, rows, :], axis=0, keepdims=True)
            )

        def visit(c, state):
            start = pl.multiple_of(c * length, length)
            for h in range(heads):
                rows = slice(h * dim, (h + 1) * dim)
                q = qkv_ref[h * dim : (h + 1) * dim, pl.ds(q_start, length)]
                g = grad_ref[j, rows, :]
                s = dot_f32(k3[h, pl.ds(start, length), :], q, ((1,), (0,)))
                s = s + bias_ref[h, block - c].astype(f32)
                p = jnp.exp(s - lse_ref[j, h : h + 1, :])
                dp = dot_f32(v3[h, pl.ds(start, length), :], g, ((1,), (0,)))
                ds = (p * (dp - state[h])).astype(bf16)
                grad_v[rows, pl.ds(start, length)] += dot_f32(g, p.astype(bf16), ((1,), (1,)))
                grad_k[rows, pl.ds(start, length)] += dot_f32(q, ds, ((1,), (1,)))
                kt = qkv_ref[third + h * dim : third + (h + 1) * dim, pl.ds(start, length)]
                grad_q[rows, :] += dot_f32(kt, ds, ((1,), (0,)))
                grad_b[h, block - c] += ds.astype(f32)
            return state

        lax.fori_loop(0, block + 1, visit, tuple(delta))
        done = (grad_q[...] * 0.125).astype(bf16)
        q_ref[j] = done
        sum_w[:third, :] += dot_f32(done, normed_ref[block], ((1,), (0,)))
    for o in range(splits):
        other = jnp.bitwise_xor(own, o)
        for j in range(groups):
            start = pl.multiple_of((j * splits + other) * length, length)
            kv_refs[o][j, :third, :] = grad_k[:, pl.ds(start, length)].astype(bf16)
            kv_refs[o][j, third:, :] = grad_v[:, pl.ds(start, length)].astype(bf16)

    def weigh(c, _):
        start = pl.multiple_of(c * length, length)
        seen = normed_ref[c]
        sum_w[third : 2 * third, :] += dot_f32(grad_k[:, pl.ds(start, length)].astype(bf16), seen, ((1,), (0,)))
        sum_w[2 * third :, :] += dot_f32(grad_v[:, pl.ds(start, length)].astype(bf16), seen, ((1,), (0,)))
        return 0

    lax.fori_loop(0, blocks, weigh, 0)
    row = lax.broadcasted_iota(jnp.int32, (8, 2 * length), 0)

    def diagonals(d, _):
        for h in range(heads):
            tile = grad_b[h, d]
            tile = jnp.concatenate([jnp.zeros_like(tile), tile], axis=1)
            size = length // 2
            while size >= 8:
                tile = tile[:size] + pltpu.roll(tile[size:], 2 * length - size, 1)
                size //= 2
            for bit in (1, 2, 4):
                tile = jnp.where((row & bit) != 0, pltpu.roll(tile, 2 * length - bit, 1), tile)
            diag_ref[d, h : h + 1, :] = jnp.sum(tile, axis=0, keepdims=True)
        return 0

    lax.fori_loop(0, blocks, diagonals, 0)

    def by_bucket(d, total):
        start = pl.multiple_of(d * length, length)
        summed = diag_ref[d, :, length:]
        nearer = diag_ref[jnp.minimum(d + 1, blocks - 1), :, :length]
        summed = summed + jnp.where(d + 1 < blocks, 1.0, 0.0) * nearer
        return total + lax.dot_general(
            summed, named_ref[pl.ds(start, length), :], (((1,), (0,)), ((), ())),
            preferred_element_type=f32, precision=lax.Precision.HIGHEST,
        )

    diag_ref[:, heads:, :] = jnp.zeros((blocks, 8 - heads, 2 * length), f32)
    buckets = lax.fori_loop(0, blocks, by_bucket, jnp.zeros((8, named_ref.shape[1]), f32))
    made = sum_w[...]
    gain_grad = jnp.sum(made * weight_ref[...].astype(f32), axis=0, keepdims=True) / gain_ref[...]
    shares, small_rows, share = small_ref.shape
    size = 3 * third
    at = lax.broadcasted_iota(jnp.int32, (small_rows, share), 0)
    first_row = own_ref[1]
    each = named_ref.shape[1] // shares
    for d in range(shares):
        parts_ref[d, :size, :] = made[:, d * share : (d + 1) * share].astype(bf16)
        small = small_ref[d]
        small = small + jnp.where(at == own_ref[2], gain_grad[:, d * share : (d + 1) * share], 0.0)
        for h in range(heads):
            line = jnp.concatenate(
                [buckets[h : h + 1, d * each : (d + 1) * each], jnp.zeros((1, share - each), f32)], axis=1
            )
            small = small + jnp.where(at == first_row + h, line, 0.0)
        parts_ref[d, size:, :] = small.astype(bf16)


def attend_back(own, qkv, tiles, grad_context, wide, lse, normed, weight, gain, named, small, groups, splits):
    heads, blocks, length, _ = tiles.shape
    third = qkv.shape[0] // 3
    dim = third // heads
    vmem = pl.BlockSpec(memory_space=pltpu.VMEM)
    units = heads * groups * (blocks + 1) // 2
    shares, small_rows, share = small.shape
    return pl.pallas_call(
        functools.partial(attend_back_kernel, heads, groups, splits),
        in_specs=[pl.BlockSpec(memory_space=pltpu.SMEM)] + [vmem] * 10,
        out_specs=[vmem] * (2 + splits),
        out_shape=[jax.ShapeDtypeStruct((groups, third, length), bf16)]
        + [jax.ShapeDtypeStruct((groups, 2 * third, length), bf16)] * splits
        + [jax.ShapeDtypeStruct((shares, 3 * third + small_rows, share), bf16)],
        scratch_shapes=[
            pltpu.VMEM((blocks, 8, 2 * length), f32),
            pltpu.VMEM(weight.shape, f32),
            pltpu.VMEM((heads, blocks * length, dim), bf16),
            pltpu.VMEM((heads, blocks * length, dim), bf16),
            pltpu.VMEM((third, blocks * length), f32),
            pltpu.VMEM((third, blocks * length), f32),
            pltpu.VMEM((third, length), f32),
            pltpu.VMEM((heads, blocks, length, length), f32),
        ],
        compiler_params=pltpu.CompilerParams(vmem_limit_bytes=vmem_bytes),
        cost_estimate=pl.CostEstimate(
            flops=units * length * length * 256 * 10,
            bytes_accessed=20 * 1024 * 1024,
            transcendentals=units * length * length,
        ),
        name="attend_back",
    )(own, qkv, tiles, grad_context, wide, lse, normed, weight, gain, named, small)


def expert_kernel(
    experts, top, own_ref, xa_ref, xb_ref, ua_ref, ub_ref, router_ref, weight_ref,
    mixed_a, mixed_b, gx_a, gx_b, gg_a, gg_b, grad_ref, sum_rows, sum_gx, sum_grad, g_rows, gates,
):
    step = pl.program_id(0)
    near = xa_ref.shape[0]
    units = weight_ref.shape[1] // 2
    tile = min(near, 512)
    root = 0.7978845608028654
    places = [
        (half * near + at, half, slice(at, at + tile), slice(half * near + at, half * near + at + tile))
        for half in range(2)
        for at in range(0, near, tile)
    ]
    lane = lax.broadcasted_iota(jnp.int32, (tile, 128), 1)
    own = own_ref[0]

    @pl.when(step == 0)
    def _():
        sum_rows[...] = jnp.zeros_like(sum_rows)
        sum_gx[...] = jnp.zeros_like(sum_gx)
        for _, half, part, whole in places:
            x = (xa_ref, xb_ref)[half][part, :]
            width = x.shape[1]
            routes = (ua_ref, ub_ref)[half][part, width:].astype(jnp.int32)
            logits = dot_f32(x, router_ref[...], ((1,), (1,)))
            logits = jnp.where(lane < experts, logits, masked_score)
            chances = jnp.exp(logits - jnp.max(logits, axis=1, keepdims=True))
            chances = chances / jnp.sum(chances, axis=1, keepdims=True)
            select = jnp.zeros((tile, 128), f32)
            for k in range(top):
                select = select + jnp.where(lane == routes[:, k : k + 1], 1.0, 0.0)
            picked = select * chances
            mine = jnp.where(lane == own, 1.0, 0.0)
            gate = jnp.sum(mine * picked, axis=1, keepdims=True) / jnp.sum(picked, axis=1, keepdims=True)
            routed = jnp.sum(mine * select, axis=1, keepdims=True)
            gates[whole, :] = jnp.where(lane == 0, gate, routed)
            u = (ua_ref, ub_ref)[half][part, :width].astype(f32)
            g_rows[whole, :] = (gate * u).astype(bf16)

    first = weight_ref[0, :units, :]
    second = weight_ref[0, units:, :]
    for start, half, part, whole in places:
        x = (xa_ref, xb_ref)[half][part, :]
        g = g_rows[whole, :]
        pre = dot_f32(x, first, ((1,), (1,)))
        back = dot_f32(g, second, ((1,), (1,)))
        square = pre * pre
        bent = jnp.tanh(pre * (root + (root * 0.044715) * square))
        halved = 0.5 + 0.5 * bent
        active = pre * halved
        hidden = active.astype(bf16)
        slope = halved + active * (1.0 - bent) * (root + (root * 0.134145) * square)
        gp = (back * slope).astype(bf16)
        sum_rows[whole, :] += dot_f32(hidden, second, ((1,), (0,)))
        sum_gx[whole, :] += dot_f32(gp, first, ((1,), (0,)))
        grad_first = dot_f32(gp, x, ((0,), (0,)))
        grad_second = dot_f32(hidden, g, ((0,), (0,)))
        if start == 0:
            sum_grad[:units, :] = grad_first
            sum_grad[units:, :] = grad_second
        else:
            sum_grad[:units, :] += grad_first
            sum_grad[units:, :] += grad_second
    grad_ref[0] = sum_grad[...].astype(bf16)

    @pl.when(step == pl.num_programs(0) - 1)
    def _():
        for _, half, part, whole in places:
            result = sum_rows[whole, :].astype(bf16).astype(f32)
            gate = gates[whole, 0:1]
            routed = gates[whole, 1:2]
            u = (ua_ref, ub_ref)[half][part, : result.shape[1]].astype(f32)
            dots = jnp.sum(u * result, axis=1, keepdims=True) * routed
            (gg_a, gg_b)[half][part, :] = jnp.where(lane == own, dots, 0.0)
            (mixed_a, mixed_b)[half][part, :] = (gate * result).astype(bf16)
            (gx_a, gx_b)[half][part, :] = jnp.where(routed > 0.5, sum_gx[whole, :], 0.0).astype(bf16)


def run_expert(own, x, u, router, experts, top, weights):
    rows, width = x[0].shape
    shards, units = weights.shape[0], weights.shape[1] // 2

    def whole(array):
        return pl.BlockSpec(array.shape, lambda i: (0, 0), pipeline_mode=pl.Buffered(1))

    def rows_of(columns):
        return pl.BlockSpec((rows, columns), lambda i: (0, 0))

    shard_spec = pl.BlockSpec((1, 2 * units, width), lambda i: (i, 0, 0))
    operands = (*x, *u, router)
    return pl.pallas_call(
        functools.partial(expert_kernel, experts, top),
        grid=(shards,),
        in_specs=[pl.BlockSpec(memory_space=pltpu.SMEM)] + [whole(item) for item in operands] + [shard_spec],
        out_specs=[rows_of(width)] * 4 + [rows_of(128)] * 2 + [shard_spec],
        out_shape=[jax.ShapeDtypeStruct((rows, width), bf16)] * 4
        + [jax.ShapeDtypeStruct((rows, 128), f32)] * 2
        + [jax.ShapeDtypeStruct(weights.shape, bf16)],
        scratch_shapes=[pltpu.VMEM((2 * rows, width), f32)] * 2
        + [
            pltpu.VMEM((2 * units, width), f32),
            pltpu.VMEM((2 * rows, width), bf16),
            pltpu.VMEM((2 * rows, 128), f32),
        ],
        compiler_params=pltpu.CompilerParams(vmem_limit_bytes=vmem_bytes),
        cost_estimate=pl.CostEstimate(
            flops=24 * rows * width * units * shards,
            bytes_accessed=16 * rows * width + 8 * shards * width * units,
            transcendentals=2 * rows * units * shards,
        ),
        name="run_expert",
    )(own, *operands, weights)


def order_kernel(count, third, group_ref, *refs):
    held, (q_ref, k_ref, v_ref, small_ref), placed = refs[:count], refs[count : count + 4], refs[count + 4]
    share = q_ref.shape[0]
    group = group_ref[0]
    small = None
    for s in range(count):
        placed[(group + s) % count] = held[s][: 3 * third, :]
        term = held[s][3 * third :, :].astype(f32)
        small = term if small is None else small + term
    small_ref[...] = small
    row = lax.broadcasted_iota(jnp.int32, (share, share), 0)
    column = lax.broadcasted_iota(jnp.int32, (share, share), 1)
    unit = jnp.where(row == column, 1.0, 0.0).astype(bf16)
    for g in range(count):
        for k, out_ref in enumerate((q_ref, k_ref, v_ref)):
            turned = dot_f32(unit, placed[g, k * third : (k + 1) * third, :], ((1,), (1,)))
            out_ref[:, g * third : (g + 1) * third] = turned


def put_in_order(group, held, third):
    count = len(held)
    rows, share = held[0].shape
    vmem = pl.BlockSpec(memory_space=pltpu.VMEM)
    return pl.pallas_call(
        functools.partial(order_kernel, count, third),
        in_specs=[pl.BlockSpec(memory_space=pltpu.SMEM)] + [vmem] * count,
        out_specs=[vmem] * 4,
        out_shape=[jax.ShapeDtypeStruct((share, count * third), f32)] * 3
        + [jax.ShapeDtypeStruct((rows - 3 * third, share), f32)],
        scratch_shapes=[pltpu.VMEM((count, 3 * third, share), bf16)],
        compiler_params=pltpu.CompilerParams(vmem_limit_bytes=vmem_bytes),
        name="put_in_order",
    )(group, *held)


def norm_back(x, gain, grad):
    scale = lax.rsqrt(jnp.mean(x * x, axis=-1, keepdims=True) + eps_norm)
    weighted = grad * gain
    inner = jnp.mean(weighted * x, axis=-1, keepdims=True)
    return scale * weighted - x * (scale * scale * scale) * inner, jnp.sum(grad * x * scale, axis=0)


def body(
    tokens, cotangent, w_query, w_key, w_value, attention_output_weight, router, norm1_gain, norm2_gain,
    attn_bias, w_in, w_out, routes, buckets,
):
    n_ctx = lax.axis_size("ctx")
    n_dp = lax.axis_size("dp")
    ctx_at = lax.axis_index("ctx")
    dp_at = lax.axis_index("dp")
    half = n_ctx // 2
    _, length, width = tokens.shape
    all_heads = attn_bias.shape[1]
    bucket_count = attn_bias.shape[0] * n_dp
    experts = router.shape[1]
    groups = 4
    splits = n_ctx // groups
    heads = all_heads // groups
    dim = width // all_heads
    third = heads * dim
    group_at = ctx_at // splits
    split_at = ctx_at % splits
    rows_dp = w_query.shape[0]

    tok_same, tok_across = gather_ctx([tokens[0]])
    tokens_held = [entry[0] for entry in tok_same + tok_across]
    table_size = attn_bias.shape[0] * all_heads
    table_columns = -(-table_size // rows_dp)
    table = jnp.pad(attn_bias.reshape(-1), (0, table_columns * rows_dp - table_size)).reshape(table_columns, rows_dp).T
    behind = jnp.concatenate([router, norm1_gain[:, None], norm2_gain[:, None], table], axis=1)
    behind = jnp.pad(behind, ((0, 0), (0, 128 - behind.shape[1])))
    packed = jnp.concatenate([w_query, w_key, w_value, attention_output_weight, behind], axis=1)
    packed = in_order(gather_dp(packed, tok_same), dp_at)
    dense = jnp.concatenate([item[:, : 4 * width] for item in packed], axis=0)
    behind = jnp.concatenate([item[:, 4 * width :] for item in packed], axis=0)
    output_weight = dense[:, 3 * width :]
    own_columns = [
        lax.dynamic_slice_in_dim(dense, k * width + group_at * third, third, axis=1).T for k in range(3)
    ]
    qkv_weight = jnp.concatenate(own_columns, axis=0)
    small_t = behind.T
    router_weight = small_t[:experts]
    gain_first = small_t[experts : experts + 1].astype(f32)
    gain_second = small_t[experts + 1 : experts + 2].astype(f32)
    bias_table = small_t[experts + 2 : experts + 2 + table_columns].reshape(table_columns, n_dp, rows_dp)
    bias_table = bias_table.transpose(1, 0, 2).reshape(n_dp, -1)[:, :table_size].reshape(bucket_count, all_heads)

    units = w_in.shape[2]
    z_groups = [[2 * z + x for z in range(half)] for x in range(2)]
    expert_part, _ = lax.optimization_barrier((jnp.concatenate([w_in[0].T, w_out[0]], axis=0), tok_same))
    expert_weights = lax.all_gather(expert_part, "ctx", axis=0, axis_index_groups=z_groups)

    onehot = (buckets[:, None] == jnp.arange(bucket_count, dtype=jnp.int32)[None, :]).astype(bf16)
    bias_own = lax.dynamic_slice_in_dim(bias_table, group_at * heads, heads, axis=1)
    per_distance = dot_f32(bias_own, onehot, ((0,), (1,)))
    vec = jnp.concatenate([jnp.full((heads, length), masked_score, f32), per_distance], axis=1)
    vec = jnp.pad(vec, ((0, 8 - heads), (0, 0)))
    tiles = bias_tiles(vec, heads, n_ctx, length)

    z_at, x_at = ctx_at // 2, ctx_at % 2
    places = jnp.stack(
        [((z_at - s) % half) * 2 + x_at for s in range(half)]
        + [((z_at - s) % half) * 2 + (1 - x_at) for s in range(half)]
    ).astype(jnp.int32)
    qkv_weight, tiles = lax.optimization_barrier((qkv_weight, tiles))
    normed, qkv = project(tokens_held, places, gain_first, qkv_weight)
    upstream = jnp.pad(routes[0].astype(bf16), ((0, 0), (0, 128 - routes.shape[2])))
    upstream = jnp.concatenate([cotangent[0], upstream], axis=1)
    upstream, qkv = lax.optimization_barrier((upstream, qkv))
    upstream_rows = gather_rows(upstream)
    own_split = split_at.astype(jnp.int32).reshape(1)
    low, wide, lse = attend(own_split, qkv, tiles, groups, splits)
    index_groups = [[g * splits + b for g in range(groups)] for b in range(splits)]
    context_t = lax.all_to_all(
        low, "ctx", split_axis=0, concat_axis=0, tiled=True, axis_index_groups=index_groups
    ).reshape(width, length)
    context_t, upstream_rows = lax.optimization_barrier((context_t, upstream_rows))

    resid_in = tokens[0].astype(f32)
    residual = resid_in + dot_f32(context_t, output_weight, ((0,), (0,)))
    scale2 = lax.rsqrt(jnp.mean(residual * residual, axis=-1, keepdims=True) + eps_norm)
    second = (residual * scale2 * gain_second).astype(bf16)
    second_rows = gather_rows(second)

    def gate(rows, pairs):
        logits = dot_f32(rows, router_weight, ((1,), (1,)))
        shifted = jnp.exp(logits - jnp.max(logits, axis=-1, keepdims=True))
        chances = shifted / jnp.sum(shifted, axis=-1, keepdims=True)
        named = jnp.arange(experts, dtype=jnp.int32)[None, :]
        select = jnp.zeros(chances.shape, f32)
        for k in range(pairs.shape[1]):
            select = select + (pairs[:, k : k + 1] == named).astype(f32)
        total = jnp.sum(select * chances, axis=-1, keepdims=True)
        return chances, select, total

    own_expert = dp_at.astype(jnp.int32).reshape(1)
    router_wide = jnp.pad(router_weight, ((0, 128 - experts), (0, 0)))
    near = second_rows[0].shape[0]
    chunk = min(near, 1024)
    if chunk == near:
        made = run_expert(own_expert, second_rows, upstream_rows, router_wide, experts, routes.shape[2], expert_weights)
        grad_expert = made[6]
    else:

        def one_chunk(c, state):
            def cut(held):
                return lax.dynamic_slice_in_dim(held, c * chunk, chunk, axis=0)

            def put(held, new):
                return lax.dynamic_update_slice(held, new, (c * chunk, 0))

            made = run_expert(
                own_expert, [cut(v) for v in state[:2]], [cut(v) for v in state[2:4]], router_wide, experts,
                routes.shape[2], expert_weights,
            )
            high = [item.astype(bf16) for item in made[4:6]]
            low = [(item - h.astype(f32)).astype(bf16) for item, h in zip(made[4:6], high)]
            wide = [
                jnp.concatenate([m, h[:, :64], lo[:, :64]], axis=1) for m, h, lo in zip(made[0:2], high, low)
            ]
            order = (made[2], made[3], wide[0], wide[1])
            summed = (state[4].astype(f32) + made[6].astype(f32)).astype(bf16)
            return tuple(put(v, new) for v, new in zip(state[:4], order)) + (summed,)

        start = (*second_rows, *upstream_rows, jnp.zeros(expert_weights.shape, bf16))
        done = lax.fori_loop(0, near // chunk, one_chunk, start)
        made = [done[2][:, :width], done[3][:, :width], done[0], done[1]]
        made += [v[:, width : width + 64].astype(f32) + v[:, width + 64 :].astype(f32) for v in done[2:4]]
        grad_expert = done[4]
    mixed, grad_dispatched = made[0:2], made[2:4]
    grad_gate_rows = [item[:, :experts] for item in made[4:6]]
    grad_expert = lax.psum_scatter(
        grad_expert, "ctx", scatter_dimension=0, tiled=False, axis_index_groups=z_groups
    ).astype(f32)
    grad_w_in = grad_expert[:units].T[None]
    grad_w_out = grad_expert[units:][None]
    moe_grad = scatter_sum_end(*scatter_sum_rows(*grad_dispatched, bf16))
    grad_gating = scatter_sum_end(*scatter_sum_rows(*grad_gate_rows, f32))

    chances, select, total = gate(second, routes[0])
    inner = jnp.sum(select * grad_gating * chances, axis=-1, keepdims=True)
    grad_chances = select * (grad_gating / total - inner / (total * total))
    grad_logits = (chances * (grad_chances - jnp.sum(chances * grad_chances, axis=-1, keepdims=True))).astype(bf16)
    grad_router = dot_f32(grad_logits, second, ((0,), (0,)))
    grad_second = moe_grad + dot_f32(grad_logits, router_weight, ((1,), (0,)))
    grad_norm, grad_gain_second = norm_back(residual, gain_second, grad_second)
    grad_residual = cotangent[0].astype(f32) + grad_norm
    grad_attn = grad_residual.astype(bf16)

    mixed, _ = lax.optimization_barrier((mixed, grad_attn))
    layer_out = (residual + scatter_sum_end(*scatter_sum_rows(*mixed, bf16))).astype(bf16)[None]

    grad_context_t = dot_f32(output_weight, grad_attn, ((1,), (1,))).astype(bf16)
    grad_context = lax.all_to_all(
        grad_context_t.reshape(groups, third, length),
        "ctx", split_axis=0, concat_axis=0, tiled=True, axis_index_groups=index_groups,
    )
    grad_output_w = dot_f32(context_t, grad_attn, ((1,), (0,))).astype(bf16)

    def share_of(device):
        return lax.dynamic_slice_in_dim(grad_output_w, device * rows_dp, rows_dp, axis=0)

    shares = [share_of(dp_at)] + [xor_move(share_of(dp_at ^ o), "dp", o) for o in range(1, n_dp)]
    grad_output_w = sum(item.astype(f32) for item in shares)
    grad_context, grad_output_w = lax.optimization_barrier((grad_context, grad_output_w))
    small_count = experts + 2 + all_heads
    small = jnp.concatenate([grad_router, jnp.zeros((1, width), f32), grad_gain_second[None]], axis=0)
    small = jnp.pad(small.reshape(experts + 2, n_dp, rows_dp).transpose(1, 0, 2), ((0, 0), (0, -(experts + 2) % 32), (0, 0)))
    small = jnp.pad(small, ((0, 0), (0, -(-small_count // 32) * 32 - small.shape[1]), (0, 0)))
    mask = 1
    while mask < n_ctx:
        grad_output_w = grad_output_w + xor_move(grad_output_w.astype(bf16), "ctx", mask).astype(f32)
        mask *= 2
    numbers = jnp.stack([split_at, experts + 2 + group_at * heads, experts + 0 * split_at]).astype(jnp.int32)
    if n_ctx > 8:
        vec, _ = lax.optimization_barrier((vec, grad_attn))
        tiles = bias_tiles(vec, heads, n_ctx, length)
    made = attend_back(
        numbers, qkv, tiles, grad_context, wide, lse, normed, qkv_weight, gain_first, onehot.astype(f32), small,
        groups, splits,
    )
    grad_q, kept, parts = made[0], list(made[1 : 1 + splits]), made[1 + splits]

    mask = splits // 2
    while mask:
        arrived = [xor_move(item, "ctx", mask) for item in kept[mask:]]
        kept = [(mine.astype(f32) + other.astype(f32)).astype(bf16) for mine, other in zip(kept[:mask], arrived)]
        mask //= 2
    own_qkv = lax.all_to_all(
        jnp.concatenate([grad_q, kept[0]], axis=1),
        "ctx", split_axis=0, concat_axis=0, tiled=True, axis_index_groups=index_groups,
    )
    parts = lax.all_to_all(parts, "dp", split_axis=0, concat_axis=0, tiled=True)
    gw = jnp.sum(parts.astype(f32), axis=0)
    mask = 1
    while mask < splits:
        gw = gw + xor_move(gw.astype(bf16), "ctx", mask).astype(f32)
        mask *= 2
    gw = gw.astype(bf16)
    held = [gw] + [shift_move(gw, "ctx", -splits * s) for s in range(1, groups)]
    grad_wq, grad_wk, grad_wv, small_grads = put_in_order(group_at.astype(jnp.int32).reshape(1), held, third)
    grad_router = small_grads[:experts].T
    grad_gain_first = small_grads[experts]
    grad_gain_second = small_grads[experts + 1]
    grad_bias = small_grads[experts + 2 : small_count, : attn_bias.shape[0]].T

    grad_normed = None
    for k in range(3):
        part = own_qkv[:, k * third : (k + 1) * third, :].reshape(width, length)
        term = dot_f32(part, dense[:, k * width : (k + 1) * width], ((0,), (1,)))
        grad_normed = term if grad_normed is None else grad_normed + term
    grad_in_norm = norm_back(resid_in, gain_first, grad_normed)[0]
    input_grad = (grad_residual + grad_in_norm)[None]
    return (
        layer_out, input_grad, grad_wq, grad_wk, grad_wv, grad_output_w, grad_router,
        grad_gain_first, grad_gain_second, grad_bias, grad_w_in, grad_w_out,
    )


def solution(mesh):
    in_specs = (
        P("dp", "ctx", None),
        P("dp", "ctx", None),
        P("dp", None),
        P("dp", None),
        P("dp", None),
        P("dp", None),
        P("dp", None),
        P("dp"),
        P("dp"),
        P("dp", None),
        P("dp", None, "ctx"),
        P("dp", "ctx", None),
        P("dp", "ctx", None),
        P(),
    )
    out_specs = (
        P("dp", "ctx", None),
        P("dp", "ctx", None),
        P("dp", None),
        P("dp", None),
        P("dp", None),
        P("dp", None),
        P("dp", None),
        P("dp"),
        P("dp"),
        P("dp", None),
        P("dp", None, "ctx"),
        P("dp", "ctx", None),
    )
    return jax.shard_map(body, mesh=mesh, in_specs=in_specs, out_specs=out_specs, check_vma=False)
```

```python
import functools

import jax
import jax.numpy as jnp
from jax import lax
from jax.experimental import pallas as pl
from jax.experimental.pallas import tpu as pltpu
from jax.sharding import PartitionSpec as P

bf16 = jnp.bfloat16
f32 = jnp.float32
eps_norm = 1e-06
masked_score = -1e30
vmem_bytes = 58 * 1024 * 1024


def dot_f32(a, b, contract):
    return lax.dot_general(a, b, (contract, ((), ())), preferred_element_type=f32)


def xor_move(value, axis, mask):
    count = lax.axis_size(axis)
    return lax.ppermute(value, axis, [(i, i ^ mask) for i in range(count)])


def shift_move(value, axis, step):
    count = lax.axis_size(axis)
    return lax.ppermute(value, axis, [(i, (i + step) % count) for i in range(count)])


def dp_offsets(count):
    offsets, mask = [0], count // 2
    while mask:
        offsets = offsets + [o ^ mask for o in offsets]
        mask //= 2
    return offsets


def gather_dp(block, after):
    count = lax.axis_size("dp")
    held, mask = [block], count // 2
    while mask:
        if mask == 1:
            held, _ = lax.optimization_barrier((held, after))
        held = held + [xor_move(item, "dp", mask) for item in held]
        mask //= 2
    return held


def in_order(held, own):
    count = len(held)
    by_offset = [None] * count
    for offset, item in zip(dp_offsets(count), held):
        by_offset[offset] = item
    mask = 1
    while mask < count:
        swap = (own & mask) != 0
        by_offset = [jnp.where(swap, by_offset[o ^ mask], by_offset[o]) for o in range(count)]
        mask *= 2
    return by_offset


def gather_rows(block, before=None, between=None):
    far = lax.axis_size("dp") // 2
    items = [block, xor_move(block, "ctx", 1)]
    if before is not None:
        items, _ = lax.optimization_barrier((items, before))
    items = items + [xor_move(item, "dp", far) for item in items]
    if between is not None:
        items, _ = lax.optimization_barrier((items, between))
    rows = jnp.concatenate(items, axis=0)
    mask = far // 2
    while mask > 1:
        rows = jnp.concatenate([rows, xor_move(rows, "dp", mask)], axis=0)
        mask //= 2
    return rows, xor_move(rows, "dp", 1)


def scatter_sum_rows(near, other, sent):
    far = lax.axis_size("dp") // 2
    rows = near.astype(f32) + xor_move(other.astype(sent), "dp", 1).astype(f32)
    rows = rows.astype(sent) if far > 2 else rows
    mask = 2
    while mask < far:
        cut = rows.shape[0] // 2
        arrived = xor_move(rows[cut:].astype(sent), "dp", mask)
        rows = (rows[:cut].astype(f32) + arrived.astype(f32)).astype(sent)
        mask *= 2
    cut = rows.shape[0] // 4
    own, over_x, over_y, over_both = [rows[k * cut : (k + 1) * cut] for k in range(4)]
    arrived = xor_move(over_both.astype(sent), "dp", far)
    over_x = (over_x.astype(f32) + arrived.astype(f32)).astype(sent)
    own = own.astype(f32) + xor_move(over_y.astype(sent), "dp", far).astype(f32)
    return own, over_x


def scatter_sum_end(own, over_x):
    return own + xor_move(over_x, "ctx", 1).astype(f32)


def gather_ctx(blocks):
    half = lax.axis_size("ctx") // 2
    same = [blocks] + [[shift_move(item, "ctx", 2 * s) for item in blocks] for s in range(1, half)]
    across = [[xor_move(item, "ctx", 1) for item in entry] for entry in same]
    return same, across


def bias_kernel(vec_ref, tile_ref):
    heads, length = tile_ref.shape[0], tile_ref.shape[2]
    d = pl.program_id(0)
    start = pl.multiple_of(d * length, length)
    rows = lax.broadcasted_iota(jnp.int32, (8, 2 * length), 0)
    for h in range(heads):
        base = vec_ref[h : h + 1, pl.ds(start, 2 * length)]
        tile = jnp.broadcast_to(base, (8, 2 * length))
        for bit in (1, 2, 4):
            tile = jnp.where((rows & bit) != 0, pltpu.roll(tile, bit, 1), tile)
        size = 8
        while size < length:
            tile = jnp.concatenate([tile, pltpu.roll(tile, size, 1)], axis=0)
            size *= 2
        tile_ref[h, 0] = tile[:, length:].astype(bf16)


def bias_tiles(vec, heads, blocks, length):
    return pl.pallas_call(
        bias_kernel,
        grid=(blocks,),
        in_specs=[pl.BlockSpec(vec.shape, lambda d: (0, 0))],
        out_specs=pl.BlockSpec((heads, 1, length, length), lambda d: (0, d, 0, 0)),
        out_shape=jax.ShapeDtypeStruct((heads, blocks, length, length), bf16),
        compiler_params=pltpu.CompilerParams(vmem_limit_bytes=vmem_bytes),
        name="bias_tiles",
    )(vec)


def qkv_kernel(count, place_ref, gain_ref, weight_ref, *refs):
    token_refs, (normed_ref, out_ref) = refs[:count], refs[count:]
    length = token_refs[0].shape[0]
    third = weight_ref.shape[0] // 3
    for r in range(count):
        place = place_ref[r]
        start = pl.multiple_of(place * length, length)
        x = token_refs[r][...].astype(f32)
        scale = lax.rsqrt(jnp.mean(x * x, axis=-1, keepdims=True) + eps_norm)
        normed = (x * scale * gain_ref[...]).astype(bf16)
        normed_ref[place] = normed
        made = dot_f32(weight_ref[...], normed, ((1,), (1,))).astype(bf16)
        out_ref[:third, pl.ds(start, length)] = (made[:third].astype(f32) * 0.125).astype(bf16)
        out_ref[third:, pl.ds(start, length)] = made[third:]


def project(tokens_held, places, gain, weight):
    count = len(tokens_held)
    length, width = tokens_held[0].shape
    vmem = pl.BlockSpec(memory_space=pltpu.VMEM)
    return pl.pallas_call(
        functools.partial(qkv_kernel, count),
        in_specs=[pl.BlockSpec(memory_space=pltpu.SMEM)] + [vmem] * (count + 2),
        out_specs=[vmem, vmem],
        out_shape=[
            jax.ShapeDtypeStruct((count, length, width), bf16),
            jax.ShapeDtypeStruct((weight.shape[0], count * length), bf16),
        ],
        compiler_params=pltpu.CompilerParams(vmem_limit_bytes=vmem_bytes),
        cost_estimate=pl.CostEstimate(
            flops=2 * count * length * width * weight.shape[0],
            bytes_accessed=2 * count * length * (2 * width + weight.shape[0]),
            transcendentals=0,
        ),
        name="project",
    )(places, gain, weight, *tokens_held)


def attend_kernel(heads, groups, splits, own_ref, qkv_ref, bias_ref, low_ref, wide_ref, lse_ref, k3, acc):
    length = bias_ref.shape[2]
    blocks = bias_ref.shape[1]
    dim = k3.shape[2]
    third = heads * dim
    for h in range(heads):

        def turn(c, _):
            start = pl.multiple_of(c * length, length)
            k3[h, pl.ds(start, length), :] = qkv_ref[
                third + h * dim : third + (h + 1) * dim, pl.ds(start, length)
            ].T
            return 0

        lax.fori_loop(0, blocks, turn, 0)
    own = own_ref[0]
    for j in range(groups):
        block = j * splits + own
        q_start = pl.multiple_of(block * length, length)
        acc[...] = jnp.zeros_like(acc)

        def visit(c, state):
            start = pl.multiple_of(c * length, length)
            out = []
            for h in range(heads):
                top, total = state[h]
                q = qkv_ref[h * dim : (h + 1) * dim, pl.ds(q_start, length)]
                s = dot_f32(k3[h, pl.ds(start, length), :], q, ((1,), (0,)))
                s = s + bias_ref[h, block - c].astype(f32)
                new_top = jnp.maximum(top, jnp.max(s, axis=0, keepdims=True))
                p = jnp.exp(s - new_top)
                fade = jnp.exp(top - new_top)
                total = total * fade + jnp.sum(p, axis=0, keepdims=True)
                v = qkv_ref[2 * third + h * dim : 2 * third + (h + 1) * dim, pl.ds(start, length)]
                acc[h] = acc[h] * fade + dot_f32(v, p.astype(bf16), ((1,), (0,)))
                out.append((new_top, total))
            return tuple(out)

        begin = tuple(
            (jnp.full((1, length), masked_score, f32), jnp.zeros((1, length), f32)) for _ in range(heads)
        )
        state = lax.fori_loop(0, block + 1, visit, begin)
        for h in range(heads):
            top, total = state[h]
            context = acc[h] / total
            wide_ref[j, h * dim : (h + 1) * dim, :] = context
            low_ref[j, h * dim : (h + 1) * dim, :] = context.astype(bf16)
            lse_ref[j, h : h + 1, :] = top + jnp.log(total)


def attend(own, qkv, tiles, groups, splits):
    heads, blocks, length, _ = tiles.shape
    third = qkv.shape[0] // 3
    dim = third // heads
    vmem = pl.BlockSpec(memory_space=pltpu.VMEM)
    units = heads * groups * (blocks + 1) // 2
    return pl.pallas_call(
        functools.partial(attend_kernel, heads, groups, splits),
        in_specs=[pl.BlockSpec(memory_space=pltpu.SMEM), vmem, vmem],
        out_specs=[vmem] * 3,
        out_shape=[
            jax.ShapeDtypeStruct((groups, third, length), bf16),
            jax.ShapeDtypeStruct((groups, third, length), f32),
            jax.ShapeDtypeStruct((groups, 8, length), f32),
        ],
        scratch_shapes=[pltpu.VMEM((heads, blocks * length, dim), bf16), pltpu.VMEM((heads, dim, length), f32)],
        compiler_params=pltpu.CompilerParams(vmem_limit_bytes=vmem_bytes),
        cost_estimate=pl.CostEstimate(
            flops=units * length * length * 256 * 4,
            bytes_accessed=10 * 1024 * 1024,
            transcendentals=units * length * length,
        ),
        name="attend",
    )(own, qkv, tiles)


def attend_back_kernel(
    heads, groups, splits, own_ref, qkv_ref, bias_ref, grad_ref, wide_ref, lse_ref, normed_ref, weight_ref,
    gain_ref, named_ref, small_ref, q_ref, *refs,
):
    kv_refs, parts_ref = refs[:splits], refs[splits]
    diag_ref, sum_w, k3, v3, grad_k, grad_v, grad_q, grad_b = refs[splits + 1 :]
    length = bias_ref.shape[2]
    blocks = bias_ref.shape[1]
    dim = k3.shape[2]
    third = heads * dim
    for h in range(heads):

        def turn(c, _):
            start = pl.multiple_of(c * length, length)
            k3[h, pl.ds(start, length), :] = qkv_ref[
                third + h * dim : third + (h + 1) * dim, pl.ds(start, length)
            ].T
            v3[h, pl.ds(start, length), :] = qkv_ref[
                2 * third + h * dim : 2 * third + (h + 1) * dim, pl.ds(start, length)
            ].T
            grad_b[h, c] = jnp.zeros((length, length), f32)
            return 0

        lax.fori_loop(0, blocks, turn, 0)
    sum_w[...] = jnp.zeros_like(sum_w)
    grad_k[...] = jnp.zeros_like(grad_k)
    grad_v[...] = jnp.zeros_like(grad_v)
    own = own_ref[0]
    for j in range(groups):
        block = j * splits + own
        q_start = pl.multiple_of(block * length, length)
        grad_q[...] = jnp.zeros_like(grad_q)
        delta = []
        for h in range(heads):
            rows = slice(h * dim, (h + 1) * dim)
            delta.append(
                jnp.sum(grad_ref[j, rows, :].astype(f32) * wide_ref[j, rows, :], axis=0, keepdims=True)
            )

        def visit(c, state):
            start = pl.multiple_of(c * length, length)
            for h in range(heads):
                rows = slice(h * dim, (h + 1) * dim)
                q = qkv_ref[h * dim : (h + 1) * dim, pl.ds(q_start, length)]
                g = grad_ref[j, rows, :]
                s = dot_f32(k3[h, pl.ds(start, length), :], q, ((1,), (0,)))
                s = s + bias_ref[h, block - c].astype(f32)
                p = jnp.exp(s - lse_ref[j, h : h + 1, :])
                dp = dot_f32(v3[h, pl.ds(start, length), :], g, ((1,), (0,)))
                ds = (p * (dp - state[h])).astype(bf16)
                grad_v[rows, pl.ds(start, length)] += dot_f32(g, p.astype(bf16), ((1,), (1,)))
                grad_k[rows, pl.ds(start, length)] += dot_f32(q, ds, ((1,), (1,)))
                kt = qkv_ref[third + h * dim : third + (h + 1) * dim, pl.ds(start, length)]
                grad_q[rows, :] += dot_f32(kt, ds, ((1,), (0,)))
                grad_b[h, block - c] += ds.astype(f32)
            return state

        lax.fori_loop(0, block + 1, visit, tuple(delta))
        done = (grad_q[...] * 0.125).astype(bf16)
        q_ref[j] = done
        sum_w[:third, :] += dot_f32(done, normed_ref[block], ((1,), (0,)))
    for o in range(splits):
        other = jnp.bitwise_xor(own, o)
        for j in range(groups):
            start = pl.multiple_of((j * splits + other) * length, length)
            kv_refs[o][j, :third, :] = grad_k[:, pl.ds(start, length)].astype(bf16)
            kv_refs[o][j, third:, :] = grad_v[:, pl.ds(start, length)].astype(bf16)

    def weigh(c, _):
        start = pl.multiple_of(c * length, length)
        seen = normed_ref[c]
        sum_w[third : 2 * third, :] += dot_f32(grad_k[:, pl.ds(start, length)].astype(bf16), seen, ((1,), (0,)))
        sum_w[2 * third :, :] += dot_f32(grad_v[:, pl.ds(start, length)].astype(bf16), seen, ((1,), (0,)))
        return 0

    lax.fori_loop(0, blocks, weigh, 0)
    row = lax.broadcasted_iota(jnp.int32, (8, 2 * length), 0)

    def diagonals(d, _):
        for h in range(heads):
            tile = grad_b[h, d]
            tile = jnp.concatenate([jnp.zeros_like(tile), tile], axis=1)
            size = length // 2
            while size >= 8:
                tile = tile[:size] + pltpu.roll(tile[size:], 2 * length - size, 1)
                size //= 2
            for bit in (1, 2, 4):
                tile = jnp.where((row & bit) != 0, pltpu.roll(tile, 2 * length - bit, 1), tile)
            diag_ref[d, h : h + 1, :] = jnp.sum(tile, axis=0, keepdims=True)
        return 0

    lax.fori_loop(0, blocks, diagonals, 0)

    def by_bucket(d, total):
        start = pl.multiple_of(d * length, length)
        summed = diag_ref[d, :, length:]
        nearer = diag_ref[jnp.minimum(d + 1, blocks - 1), :, :length]
        summed = summed + jnp.where(d + 1 < blocks, 1.0, 0.0) * nearer
        return total + lax.dot_general(
            summed, named_ref[pl.ds(start, length), :], (((1,), (0,)), ((), ())),
            preferred_element_type=f32, precision=lax.Precision.HIGHEST,
        )

    diag_ref[:, heads:, :] = jnp.zeros((blocks, 8 - heads, 2 * length), f32)
    buckets = lax.fori_loop(0, blocks, by_bucket, jnp.zeros((8, named_ref.shape[1]), f32))
    made = sum_w[...]
    gain_grad = jnp.sum(made * weight_ref[...].astype(f32), axis=0, keepdims=True) / gain_ref[...]
    shares, small_rows, share = small_ref.shape
    size = 3 * third
    at = lax.broadcasted_iota(jnp.int32, (small_rows, share), 0)
    first_row = own_ref[1]
    each = named_ref.shape[1] // shares
    for d in range(shares):
        parts_ref[d, :size, :] = made[:, d * share : (d + 1) * share].astype(bf16)
        small = small_ref[d]
        small = small + jnp.where(at == own_ref[2], gain_grad[:, d * share : (d + 1) * share], 0.0)
        for h in range(heads):
            line = jnp.concatenate(
                [buckets[h : h + 1, d * each : (d + 1) * each], jnp.zeros((1, share - each), f32)], axis=1
            )
            small = small + jnp.where(at == first_row + h, line, 0.0)
        parts_ref[d, size:, :] = small.astype(bf16)


def attend_back(own, qkv, tiles, grad_context, wide, lse, normed, weight, gain, named, small, groups, splits):
    heads, blocks, length, _ = tiles.shape
    third = qkv.shape[0] // 3
    dim = third // heads
    vmem = pl.BlockSpec(memory_space=pltpu.VMEM)
    units = heads * groups * (blocks + 1) // 2
    shares, small_rows, share = small.shape
    return pl.pallas_call(
        functools.partial(attend_back_kernel, heads, groups, splits),
        in_specs=[pl.BlockSpec(memory_space=pltpu.SMEM)] + [vmem] * 10,
        out_specs=[vmem] * (2 + splits),
        out_shape=[jax.ShapeDtypeStruct((groups, third, length), bf16)]
        + [jax.ShapeDtypeStruct((groups, 2 * third, length), bf16)] * splits
        + [jax.ShapeDtypeStruct((shares, 3 * third + small_rows, share), bf16)],
        scratch_shapes=[
            pltpu.VMEM((blocks, 8, 2 * length), f32),
            pltpu.VMEM(weight.shape, f32),
            pltpu.VMEM((heads, blocks * length, dim), bf16),
            pltpu.VMEM((heads, blocks * length, dim), bf16),
            pltpu.VMEM((third, blocks * length), f32),
            pltpu.VMEM((third, blocks * length), f32),
            pltpu.VMEM((third, length), f32),
            pltpu.VMEM((heads, blocks, length, length), f32),
        ],
        compiler_params=pltpu.CompilerParams(vmem_limit_bytes=vmem_bytes),
        cost_estimate=pl.CostEstimate(
            flops=units * length * length * 256 * 10,
            bytes_accessed=20 * 1024 * 1024,
            transcendentals=units * length * length,
        ),
        name="attend_back",
    )(own, qkv, tiles, grad_context, wide, lse, normed, weight, gain, named, small)


def expert_kernel(
    experts, top, own_ref, xa_ref, xb_ref, ua_ref, ub_ref, router_ref, weight_ref,
    mixed_a, mixed_b, gx_a, gx_b, gg_a, gg_b, grad_ref, sum_rows, sum_gx, sum_grad, g_rows, gates,
):
    step = pl.program_id(0)
    near = xa_ref.shape[0]
    joined = weight_ref.shape[0]
    units = weight_ref.shape[1] // 2
    tile = min(near, 512)
    root = 0.7978845608028654
    places = [
        (half * near + at, half, slice(at, at + tile), slice(half * near + at, half * near + at + tile))
        for half in range(2)
        for at in range(0, near, tile)
    ]
    lane = lax.broadcasted_iota(jnp.int32, (tile, 128), 1)
    own = own_ref[0]

    @pl.when(step == 0)
    def _():
        sum_rows[...] = jnp.zeros_like(sum_rows)
        sum_gx[...] = jnp.zeros_like(sum_gx)
        for _, half, part, whole in places:
            x = (xa_ref, xb_ref)[half][part, :]
            width = x.shape[1]
            routes = (ua_ref, ub_ref)[half][part, width:].astype(jnp.int32)
            logits = dot_f32(x, router_ref[...], ((1,), (1,)))
            logits = jnp.where(lane < experts, logits, masked_score)
            chances = jnp.exp(logits - jnp.max(logits, axis=1, keepdims=True))
            chances = chances / jnp.sum(chances, axis=1, keepdims=True)
            select = jnp.zeros((tile, 128), f32)
            for k in range(top):
                select = select + jnp.where(lane == routes[:, k : k + 1], 1.0, 0.0)
            picked = select * chances
            mine = jnp.where(lane == own, 1.0, 0.0)
            gate = jnp.sum(mine * picked, axis=1, keepdims=True) / jnp.sum(picked, axis=1, keepdims=True)
            routed = jnp.sum(mine * select, axis=1, keepdims=True)
            gates[whole, :] = jnp.where(lane == 0, gate, routed)
            u = (ua_ref, ub_ref)[half][part, :width].astype(f32)
            g_rows[whole, :] = (gate * u).astype(bf16)

    first = jnp.concatenate([weight_ref[k, :units, :] for k in range(joined)], axis=0)
    second = jnp.concatenate([weight_ref[k, units:, :] for k in range(joined)], axis=0)
    cut = joined * units
    for start, half, part, whole in places:
        x = (xa_ref, xb_ref)[half][part, :]
        g = g_rows[whole, :]
        pre = dot_f32(x, first, ((1,), (1,)))
        back = dot_f32(g, second, ((1,), (1,)))
        square = pre * pre
        bent = jnp.tanh(pre * (root + (root * 0.044715) * square))
        halved = 0.5 + 0.5 * bent
        active = pre * halved
        hidden = active.astype(bf16)
        slope = halved + active * (1.0 - bent) * (root + (root * 0.134145) * square)
        gp = (back * slope).astype(bf16)
        sum_rows[whole, :] += dot_f32(hidden, second, ((1,), (0,)))
        sum_gx[whole, :] += dot_f32(gp, first, ((1,), (0,)))
        grad_first = dot_f32(gp, x, ((0,), (0,)))
        grad_second = dot_f32(hidden, g, ((0,), (0,)))
        if start == 0:
            sum_grad[:cut, :] = grad_first
            sum_grad[cut:, :] = grad_second
        else:
            sum_grad[:cut, :] += grad_first
            sum_grad[cut:, :] += grad_second
    for k in range(joined):
        grad_ref[k, :units, :] = sum_grad[k * units : (k + 1) * units, :].astype(bf16)
        grad_ref[k, units:, :] = sum_grad[cut + k * units : cut + (k + 1) * units, :].astype(bf16)

    @pl.when(step == pl.num_programs(0) - 1)
    def _():
        for _, half, part, whole in places:
            result = sum_rows[whole, :].astype(bf16).astype(f32)
            gate = gates[whole, 0:1]
            routed = gates[whole, 1:2]
            u = (ua_ref, ub_ref)[half][part, : result.shape[1]].astype(f32)
            dots = jnp.sum(u * result, axis=1, keepdims=True) * routed
            (gg_a, gg_b)[half][part, :] = jnp.where(lane == own, dots, 0.0)
            (mixed_a, mixed_b)[half][part, :] = (gate * result).astype(bf16)
            (gx_a, gx_b)[half][part, :] = jnp.where(routed > 0.5, sum_gx[whole, :], 0.0).astype(bf16)


def run_expert(own, x, u, router, experts, top, weights):
    rows, width = x[0].shape
    shards, units = weights.shape[0], weights.shape[1] // 2

    def whole(array):
        return pl.BlockSpec(array.shape, lambda i: (0, 0), pipeline_mode=pl.Buffered(1))

    def rows_of(columns):
        return pl.BlockSpec((rows, columns), lambda i: (0, 0))

    joined = 2 - shards % 2
    shard_spec = pl.BlockSpec((joined, 2 * units, width), lambda i: (i, 0, 0))
    operands = (*x, *u, router)
    return pl.pallas_call(
        functools.partial(expert_kernel, experts, top),
        grid=(shards // joined,),
        in_specs=[pl.BlockSpec(memory_space=pltpu.SMEM)] + [whole(item) for item in operands] + [shard_spec],
        out_specs=[rows_of(width)] * 4 + [rows_of(128)] * 2 + [shard_spec],
        out_shape=[jax.ShapeDtypeStruct((rows, width), bf16)] * 4
        + [jax.ShapeDtypeStruct((rows, 128), f32)] * 2
        + [jax.ShapeDtypeStruct(weights.shape, bf16)],
        scratch_shapes=[pltpu.VMEM((2 * rows, width), f32)] * 2
        + [
            pltpu.VMEM((joined * 2 * units, width), f32),
            pltpu.VMEM((2 * rows, width), bf16),
            pltpu.VMEM((2 * rows, 128), f32),
        ],
        compiler_params=pltpu.CompilerParams(vmem_limit_bytes=vmem_bytes),
        cost_estimate=pl.CostEstimate(
            flops=24 * rows * width * units * shards,
            bytes_accessed=16 * rows * width + 8 * shards * width * units,
            transcendentals=2 * rows * units * shards,
        ),
        name="run_expert",
    )(own, *operands, weights)


def order_kernel(count, third, group_ref, *refs):
    held, (q_ref, k_ref, v_ref, small_ref), placed = refs[:count], refs[count : count + 4], refs[count + 4]
    share = q_ref.shape[0]
    group = group_ref[0]
    small = None
    for s in range(count):
        placed[(group + s) % count] = held[s][: 3 * third, :]
        term = held[s][3 * third :, :].astype(f32)
        small = term if small is None else small + term
    small_ref[...] = small
    row = lax.broadcasted_iota(jnp.int32, (share, share), 0)
    column = lax.broadcasted_iota(jnp.int32, (share, share), 1)
    unit = jnp.where(row == column, 1.0, 0.0).astype(bf16)
    for g in range(count):
        for k, out_ref in enumerate((q_ref, k_ref, v_ref)):
            turned = dot_f32(unit, placed[g, k * third : (k + 1) * third, :], ((1,), (1,)))
            out_ref[:, g * third : (g + 1) * third] = turned


def put_in_order(group, held, third):
    count = len(held)
    rows, share = held[0].shape
    vmem = pl.BlockSpec(memory_space=pltpu.VMEM)
    return pl.pallas_call(
        functools.partial(order_kernel, count, third),
        in_specs=[pl.BlockSpec(memory_space=pltpu.SMEM)] + [vmem] * count,
        out_specs=[vmem] * 4,
        out_shape=[jax.ShapeDtypeStruct((share, count * third), f32)] * 3
        + [jax.ShapeDtypeStruct((rows - 3 * third, share), f32)],
        scratch_shapes=[pltpu.VMEM((count, 3 * third, share), bf16)],
        compiler_params=pltpu.CompilerParams(vmem_limit_bytes=vmem_bytes),
        name="put_in_order",
    )(group, *held)


def norm_back(x, gain, grad):
    scale = lax.rsqrt(jnp.mean(x * x, axis=-1, keepdims=True) + eps_norm)
    weighted = grad * gain
    inner = jnp.mean(weighted * x, axis=-1, keepdims=True)
    return scale * weighted - x * (scale * scale * scale) * inner, jnp.sum(grad * x * scale, axis=0)


def body(
    tokens, cotangent, w_query, w_key, w_value, attention_output_weight, router, norm1_gain, norm2_gain,
    attn_bias, w_in, w_out, routes, buckets,
):
    n_ctx = lax.axis_size("ctx")
    n_dp = lax.axis_size("dp")
    ctx_at = lax.axis_index("ctx")
    dp_at = lax.axis_index("dp")
    half = n_ctx // 2
    _, length, width = tokens.shape
    all_heads = attn_bias.shape[1]
    bucket_count = attn_bias.shape[0] * n_dp
    experts = router.shape[1]
    groups = 4
    splits = n_ctx // groups
    heads = all_heads // groups
    dim = width // all_heads
    third = heads * dim
    group_at = ctx_at // splits
    split_at = ctx_at % splits
    rows_dp = w_query.shape[0]

    tok_same, tok_across = gather_ctx([tokens[0]])
    tokens_held = [entry[0] for entry in tok_same + tok_across]
    table_size = attn_bias.shape[0] * all_heads
    table_columns = -(-table_size // rows_dp)
    table = jnp.pad(attn_bias.reshape(-1), (0, table_columns * rows_dp - table_size)).reshape(table_columns, rows_dp).T
    behind = jnp.concatenate([router, norm1_gain[:, None], norm2_gain[:, None], table], axis=1)
    behind = jnp.pad(behind, ((0, 0), (0, 128 - behind.shape[1])))
    packed = jnp.concatenate([w_query, w_key, w_value, attention_output_weight, behind], axis=1)
    packed = in_order(gather_dp(packed, tok_same), dp_at)
    dense = jnp.concatenate([item[:, : 4 * width] for item in packed], axis=0)
    behind = jnp.concatenate([item[:, 4 * width :] for item in packed], axis=0)
    output_weight = dense[:, 3 * width :]
    own_columns = [
        lax.dynamic_slice_in_dim(dense, k * width + group_at * third, third, axis=1).T for k in range(3)
    ]
    qkv_weight = jnp.concatenate(own_columns, axis=0)
    small_t = behind.T
    router_weight = small_t[:experts]
    gain_first = small_t[experts : experts + 1].astype(f32)
    gain_second = small_t[experts + 1 : experts + 2].astype(f32)
    bias_table = small_t[experts + 2 : experts + 2 + table_columns].reshape(table_columns, n_dp, rows_dp)
    bias_table = bias_table.transpose(1, 0, 2).reshape(n_dp, -1)[:, :table_size].reshape(bucket_count, all_heads)

    units = w_in.shape[2]
    z_groups = [[2 * z + x for z in range(half)] for x in range(2)]
    expert_part, _ = lax.optimization_barrier((jnp.concatenate([w_in[0].T, w_out[0]], axis=0), tok_same))
    expert_weights = lax.all_gather(expert_part, "ctx", axis=0, axis_index_groups=z_groups)

    onehot = (buckets[:, None] == jnp.arange(bucket_count, dtype=jnp.int32)[None, :]).astype(bf16)
    bias_own = lax.dynamic_slice_in_dim(bias_table, group_at * heads, heads, axis=1)
    per_distance = dot_f32(bias_own, onehot, ((0,), (1,)))
    vec = jnp.concatenate([jnp.full((heads, length), masked_score, f32), per_distance], axis=1)
    vec = jnp.pad(vec, ((0, 8 - heads), (0, 0)))
    tiles = bias_tiles(vec, heads, n_ctx, length)

    z_at, x_at = ctx_at // 2, ctx_at % 2
    places = jnp.stack(
        [((z_at - s) % half) * 2 + x_at for s in range(half)]
        + [((z_at - s) % half) * 2 + (1 - x_at) for s in range(half)]
    ).astype(jnp.int32)
    qkv_weight, tiles = lax.optimization_barrier((qkv_weight, tiles))
    normed, qkv = project(tokens_held, places, gain_first, qkv_weight)
    upstream = jnp.pad(routes[0].astype(bf16), ((0, 0), (0, 128 - routes.shape[2])))
    upstream = jnp.concatenate([cotangent[0], upstream], axis=1)
    upstream, _ = lax.optimization_barrier((upstream, tok_same))
    own_split = split_at.astype(jnp.int32).reshape(1)
    low, wide, lse = attend(own_split, qkv, tiles, groups, splits)
    upstream_rows = gather_rows(upstream, qkv, low)
    index_groups = [[g * splits + b for g in range(groups)] for b in range(splits)]
    context_t = lax.all_to_all(
        low, "ctx", split_axis=0, concat_axis=0, tiled=True, axis_index_groups=index_groups
    ).reshape(width, length)
    context_t, upstream_rows = lax.optimization_barrier((context_t, upstream_rows))

    resid_in = tokens[0].astype(f32)
    residual = resid_in + dot_f32(context_t, output_weight, ((0,), (0,)))
    scale2 = lax.rsqrt(jnp.mean(residual * residual, axis=-1, keepdims=True) + eps_norm)
    second = (residual * scale2 * gain_second).astype(bf16)
    second_rows = gather_rows(second)

    def gate(rows, pairs):
        logits = dot_f32(rows, router_weight, ((1,), (1,)))
        shifted = jnp.exp(logits - jnp.max(logits, axis=-1, keepdims=True))
        chances = shifted / jnp.sum(shifted, axis=-1, keepdims=True)
        named = jnp.arange(experts, dtype=jnp.int32)[None, :]
        select = jnp.zeros(chances.shape, f32)
        for k in range(pairs.shape[1]):
            select = select + (pairs[:, k : k + 1] == named).astype(f32)
        total = jnp.sum(select * chances, axis=-1, keepdims=True)
        return chances, select, total

    own_expert = dp_at.astype(jnp.int32).reshape(1)
    router_wide = jnp.pad(router_weight, ((0, 128 - experts), (0, 0)))
    near = second_rows[0].shape[0]
    chunk = min(near, 1024)
    if chunk == near:
        made = run_expert(own_expert, second_rows, upstream_rows, router_wide, experts, routes.shape[2], expert_weights)
        grad_expert = made[6]
    else:

        def one_chunk(c, state):
            def cut(held):
                return lax.dynamic_slice_in_dim(held, c * chunk, chunk, axis=0)

            def put(held, new):
                return lax.dynamic_update_slice(held, new, (c * chunk, 0))

            made = run_expert(
                own_expert, [cut(v) for v in state[:2]], [cut(v) for v in state[2:4]], router_wide, experts,
                routes.shape[2], expert_weights,
            )
            high = [item.astype(bf16) for item in made[4:6]]
            low = [(item - h.astype(f32)).astype(bf16) for item, h in zip(made[4:6], high)]
            wide = [
                jnp.concatenate([m, h[:, :64], lo[:, :64]], axis=1) for m, h, lo in zip(made[0:2], high, low)
            ]
            order = (made[2], made[3], wide[0], wide[1])
            summed = (state[4].astype(f32) + made[6].astype(f32)).astype(bf16)
            return tuple(put(v, new) for v, new in zip(state[:4], order)) + (summed,)

        start = (*second_rows, *upstream_rows, jnp.zeros(expert_weights.shape, bf16))
        done = lax.fori_loop(0, near // chunk, one_chunk, start)
        made = [done[2][:, :width], done[3][:, :width], done[0], done[1]]
        made += [v[:, width : width + 64].astype(f32) + v[:, width + 64 :].astype(f32) for v in done[2:4]]
        grad_expert = done[4]
    mixed, grad_dispatched = made[0:2], made[2:4]
    grad_gate_rows = [item[:, :experts] for item in made[4:6]]
    grad_expert = lax.psum_scatter(
        grad_expert, "ctx", scatter_dimension=0, tiled=False, axis_index_groups=z_groups
    ).astype(f32)
    grad_w_in = grad_expert[:units].T[None]
    grad_w_out = grad_expert[units:][None]
    moe_grad = scatter_sum_end(*scatter_sum_rows(*grad_dispatched, bf16))
    grad_gating = scatter_sum_end(*scatter_sum_rows(*grad_gate_rows, f32))

    chances, select, total = gate(second, routes[0])
    inner = jnp.sum(select * grad_gating * chances, axis=-1, keepdims=True)
    grad_chances = select * (grad_gating / total - inner / (total * total))
    grad_logits = (chances * (grad_chances - jnp.sum(chances * grad_chances, axis=-1, keepdims=True))).astype(bf16)
    grad_router = dot_f32(grad_logits, second, ((0,), (0,)))
    grad_second = moe_grad + dot_f32(grad_logits, router_weight, ((1,), (0,)))
    grad_norm, grad_gain_second = norm_back(residual, gain_second, grad_second)
    grad_residual = cotangent[0].astype(f32) + grad_norm
    grad_attn = grad_residual.astype(bf16)

    mixed, _ = lax.optimization_barrier((mixed, grad_attn))
    layer_out = (residual + scatter_sum_end(*scatter_sum_rows(*mixed, bf16))).astype(bf16)[None]

    grad_context_t = dot_f32(output_weight, grad_attn, ((1,), (1,))).astype(bf16)
    grad_context = lax.all_to_all(
        grad_context_t.reshape(groups, third, length),
        "ctx", split_axis=0, concat_axis=0, tiled=True, axis_index_groups=index_groups,
    )
    grad_output_w = dot_f32(context_t, grad_attn, ((1,), (0,))).astype(bf16)

    def share_of(device):
        return lax.dynamic_slice_in_dim(grad_output_w, device * rows_dp, rows_dp, axis=0)

    shares = [share_of(dp_at)] + [xor_move(share_of(dp_at ^ o), "dp", o) for o in range(1, n_dp)]
    grad_output_w = sum(item.astype(f32) for item in shares)
    grad_context, grad_output_w = lax.optimization_barrier((grad_context, grad_output_w))
    small_count = experts + 2 + all_heads
    small = jnp.concatenate([grad_router, jnp.zeros((1, width), f32), grad_gain_second[None]], axis=0)
    small = jnp.pad(small.reshape(experts + 2, n_dp, rows_dp).transpose(1, 0, 2), ((0, 0), (0, -(experts + 2) % 32), (0, 0)))
    small = jnp.pad(small, ((0, 0), (0, -(-small_count // 32) * 32 - small.shape[1]), (0, 0)))
    mask = 1
    while mask < n_ctx:
        grad_output_w = grad_output_w + xor_move(grad_output_w.astype(bf16), "ctx", mask).astype(f32)
        mask *= 2
    numbers = jnp.stack([split_at, experts + 2 + group_at * heads, experts + 0 * split_at]).astype(jnp.int32)
    if n_ctx > 8:
        vec, _ = lax.optimization_barrier((vec, grad_attn))
        tiles = bias_tiles(vec, heads, n_ctx, length)
    made = attend_back(
        numbers, qkv, tiles, grad_context, wide, lse, normed, qkv_weight, gain_first, onehot.astype(f32), small,
        groups, splits,
    )
    grad_q, kept, parts = made[0], list(made[1 : 1 + splits]), made[1 + splits]

    mask = splits // 2
    while mask:
        arrived = [xor_move(item, "ctx", mask) for item in kept[mask:]]
        kept = [(mine.astype(f32) + other.astype(f32)).astype(bf16) for mine, other in zip(kept[:mask], arrived)]
        mask //= 2
    own_qkv = lax.all_to_all(
        jnp.concatenate([grad_q, kept[0]], axis=1),
        "ctx", split_axis=0, concat_axis=0, tiled=True, axis_index_groups=index_groups,
    )
    parts = lax.all_to_all(parts, "dp", split_axis=0, concat_axis=0, tiled=True)
    gw = jnp.sum(parts.astype(f32), axis=0)
    mask = 1
    while mask < splits:
        gw = gw + xor_move(gw.astype(bf16), "ctx", mask).astype(f32)
        mask *= 2
    gw = gw.astype(bf16)
    held = [gw] + [shift_move(gw, "ctx", -splits * s) for s in range(1, groups)]
    grad_wq, grad_wk, grad_wv, small_grads = put_in_order(group_at.astype(jnp.int32).reshape(1), held, third)
    grad_router = small_grads[:experts].T
    grad_gain_first = small_grads[experts]
    grad_gain_second = small_grads[experts + 1]
    grad_bias = small_grads[experts + 2 : small_count, : attn_bias.shape[0]].T

    grad_normed = None
    for k in range(3):
        part = own_qkv[:, k * third : (k + 1) * third, :].reshape(width, length)
        term = dot_f32(part, dense[:, k * width : (k + 1) * width], ((0,), (1,)))
        grad_normed = term if grad_normed is None else grad_normed + term
    grad_in_norm = norm_back(resid_in, gain_first, grad_normed)[0]
    input_grad = (grad_residual + grad_in_norm)[None]
    return (
        layer_out, input_grad, grad_wq, grad_wk, grad_wv, grad_output_w, grad_router,
        grad_gain_first, grad_gain_second, grad_bias, grad_w_in, grad_w_out,
    )


def solution(mesh):
    in_specs = (
        P("dp", "ctx", None),
        P("dp", "ctx", None),
        P("dp", None),
        P("dp", None),
        P("dp", None),
        P("dp", None),
        P("dp", None),
        P("dp"),
        P("dp"),
        P("dp", None),
        P("dp", None, "ctx"),
        P("dp", "ctx", None),
        P("dp", "ctx", None),
        P(),
    )
    out_specs = (
        P("dp", "ctx", None),
        P("dp", "ctx", None),
        P("dp", None),
        P("dp", None),
        P("dp", None),
        P("dp", None),
        P("dp", None),
        P("dp"),
        P("dp"),
        P("dp", None),
        P("dp", None, "ctx"),
        P("dp", "ctx", None),
    )
    return jax.shard_map(body, mesh=mesh, in_specs=in_specs, out_specs=out_specs, check_vma=False)
```

```python
import functools

import jax
import jax.numpy as jnp
from jax import lax
from jax.experimental import pallas as pl
from jax.experimental.pallas import tpu as pltpu
from jax.sharding import PartitionSpec as P

bf16 = jnp.bfloat16
f32 = jnp.float32
eps_norm = 1e-06
masked_score = -1e30
vmem_bytes = 58 * 1024 * 1024


def dot_f32(a, b, contract):
    return lax.dot_general(a, b, (contract, ((), ())), preferred_element_type=f32)


def xor_move(value, axis, mask):
    count = lax.axis_size(axis)
    return lax.ppermute(value, axis, [(i, i ^ mask) for i in range(count)])


def shift_move(value, axis, step):
    count = lax.axis_size(axis)
    return lax.ppermute(value, axis, [(i, (i + step) % count) for i in range(count)])


def dp_offsets(count):
    offsets, mask = [0], count // 2
    while mask:
        offsets = offsets + [o ^ mask for o in offsets]
        mask //= 2
    return offsets


def gather_dp(block, after):
    count = lax.axis_size("dp")
    held, mask = [block], count // 2
    while mask:
        if mask == 1:
            held, _ = lax.optimization_barrier((held, after))
        held = held + [xor_move(item, "dp", mask) for item in held]
        mask //= 2
    return held


def in_order(held, own):
    count = len(held)
    by_offset = [None] * count
    for offset, item in zip(dp_offsets(count), held):
        by_offset[offset] = item
    mask = 1
    while mask < count:
        swap = (own & mask) != 0
        by_offset = [jnp.where(swap, by_offset[o ^ mask], by_offset[o]) for o in range(count)]
        mask *= 2
    return by_offset


def gather_rows(block, before=None, between=None):
    far = lax.axis_size("dp") // 2
    items = [block, xor_move(block, "ctx", 1)]
    if before is not None:
        items, _ = lax.optimization_barrier((items, before))
    items = items + [xor_move(item, "dp", far) for item in items]
    if between is not None:
        items, _ = lax.optimization_barrier((items, between))
    rows = jnp.concatenate(items, axis=0)
    mask = far // 2
    while mask > 1:
        rows = jnp.concatenate([rows, xor_move(rows, "dp", mask)], axis=0)
        mask //= 2
    return rows, xor_move(rows, "dp", 1)


def scatter_sum_rows(near, other, sent):
    far = lax.axis_size("dp") // 2
    rows = near.astype(f32) + xor_move(other.astype(sent), "dp", 1).astype(f32)
    rows = rows.astype(sent) if far > 2 else rows
    mask = 2
    while mask < far:
        cut = rows.shape[0] // 2
        arrived = xor_move(rows[cut:].astype(sent), "dp", mask)
        rows = (rows[:cut].astype(f32) + arrived.astype(f32)).astype(sent)
        mask *= 2
    cut = rows.shape[0] // 4
    own, over_x, over_y, over_both = [rows[k * cut : (k + 1) * cut] for k in range(4)]
    arrived = xor_move(over_both.astype(sent), "dp", far)
    over_x = (over_x.astype(f32) + arrived.astype(f32)).astype(sent)
    own = own.astype(f32) + xor_move(over_y.astype(sent), "dp", far).astype(f32)
    return own, over_x


def scatter_sum_end(own, over_x):
    return own + xor_move(over_x, "ctx", 1).astype(f32)


def gather_ctx(blocks):
    half = lax.axis_size("ctx") // 2
    same = [blocks] + [[shift_move(item, "ctx", 2 * s) for item in blocks] for s in range(1, half)]
    across = [[xor_move(item, "ctx", 1) for item in entry] for entry in same]
    return same, across


def bias_kernel(vec_ref, tile_ref):
    heads, length = tile_ref.shape[0], tile_ref.shape[2]
    d = pl.program_id(0)
    start = pl.multiple_of(d * length, length)
    rows = lax.broadcasted_iota(jnp.int32, (8, 2 * length), 0)
    for h in range(heads):
        base = vec_ref[h : h + 1, pl.ds(start, 2 * length)]
        tile = jnp.broadcast_to(base, (8, 2 * length))
        for bit in (1, 2, 4):
            tile = jnp.where((rows & bit) != 0, pltpu.roll(tile, bit, 1), tile)
        size = 8
        while size < length:
            tile = jnp.concatenate([tile, pltpu.roll(tile, size, 1)], axis=0)
            size *= 2
        tile_ref[h, 0] = tile[:, length:].astype(bf16)


def bias_tiles(vec, heads, blocks, length):
    return pl.pallas_call(
        bias_kernel,
        grid=(blocks,),
        in_specs=[pl.BlockSpec(vec.shape, lambda d: (0, 0))],
        out_specs=pl.BlockSpec((heads, 1, length, length), lambda d: (0, d, 0, 0)),
        out_shape=jax.ShapeDtypeStruct((heads, blocks, length, length), bf16),
        compiler_params=pltpu.CompilerParams(vmem_limit_bytes=vmem_bytes),
        name="bias_tiles",
    )(vec)


def qkv_kernel(count, place_ref, gain_ref, weight_ref, *refs):
    token_refs, (normed_ref, out_ref) = refs[:count], refs[count:]
    length = token_refs[0].shape[0]
    third = weight_ref.shape[0] // 3
    for r in range(count):
        place = place_ref[r]
        start = pl.multiple_of(place * length, length)
        x = token_refs[r][...].astype(f32)
        scale = lax.rsqrt(jnp.mean(x * x, axis=-1, keepdims=True) + eps_norm)
        normed = (x * scale * gain_ref[...]).astype(bf16)
        normed_ref[place] = normed
        made = dot_f32(weight_ref[...], normed, ((1,), (1,))).astype(bf16)
        out_ref[:third, pl.ds(start, length)] = (made[:third].astype(f32) * 0.125).astype(bf16)
        out_ref[third:, pl.ds(start, length)] = made[third:]


def project(tokens_held, places, gain, weight):
    count = len(tokens_held)
    length, width = tokens_held[0].shape
    vmem = pl.BlockSpec(memory_space=pltpu.VMEM)
    return pl.pallas_call(
        functools.partial(qkv_kernel, count),
        in_specs=[pl.BlockSpec(memory_space=pltpu.SMEM)] + [vmem] * (count + 2),
        out_specs=[vmem, vmem],
        out_shape=[
            jax.ShapeDtypeStruct((count, length, width), bf16),
            jax.ShapeDtypeStruct((weight.shape[0], count * length), bf16),
        ],
        compiler_params=pltpu.CompilerParams(vmem_limit_bytes=vmem_bytes),
        cost_estimate=pl.CostEstimate(
            flops=2 * count * length * width * weight.shape[0],
            bytes_accessed=2 * count * length * (2 * width + weight.shape[0]),
            transcendentals=0,
        ),
        name="project",
    )(places, gain, weight, *tokens_held)


def attend_kernel(heads, groups, splits, own_ref, qkv_ref, bias_ref, low_ref, wide_ref, lse_ref, k3, acc):
    length = bias_ref.shape[2]
    blocks = bias_ref.shape[1]
    dim = k3.shape[2]
    third = heads * dim
    for h in range(heads):

        def turn(c, _):
            start = pl.multiple_of(c * length, length)
            k3[h, pl.ds(start, length), :] = qkv_ref[
                third + h * dim : third + (h + 1) * dim, pl.ds(start, length)
            ].T
            return 0

        lax.fori_loop(0, blocks, turn, 0)
    own = own_ref[0]
    for j in range(groups):
        block = j * splits + own
        q_start = pl.multiple_of(block * length, length)
        acc[...] = jnp.zeros_like(acc)

        def visit(c, state):
            start = pl.multiple_of(c * length, length)
            out = []
            for h in range(heads):
                top, total = state[h]
                q = qkv_ref[h * dim : (h + 1) * dim, pl.ds(q_start, length)]
                s = dot_f32(k3[h, pl.ds(start, length), :], q, ((1,), (0,)))
                s = s + bias_ref[h, block - c].astype(f32)
                new_top = jnp.maximum(top, jnp.max(s, axis=0, keepdims=True))
                p = jnp.exp(s - new_top)
                fade = jnp.exp(top - new_top)
                total = total * fade + jnp.sum(p, axis=0, keepdims=True)
                v = qkv_ref[2 * third + h * dim : 2 * third + (h + 1) * dim, pl.ds(start, length)]
                acc[h] = acc[h] * fade + dot_f32(v, p.astype(bf16), ((1,), (0,)))
                out.append((new_top, total))
            return tuple(out)

        begin = tuple(
            (jnp.full((1, length), masked_score, f32), jnp.zeros((1, length), f32)) for _ in range(heads)
        )
        state = lax.fori_loop(0, block + 1, visit, begin)
        for h in range(heads):
            top, total = state[h]
            context = acc[h] / total
            wide_ref[j, h * dim : (h + 1) * dim, :] = context
            low_ref[j, h * dim : (h + 1) * dim, :] = context.astype(bf16)
            lse_ref[j, h : h + 1, :] = top + jnp.log(total)


def attend(own, qkv, tiles, groups, splits):
    heads, blocks, length, _ = tiles.shape
    third = qkv.shape[0] // 3
    dim = third // heads
    vmem = pl.BlockSpec(memory_space=pltpu.VMEM)
    units = heads * groups * (blocks + 1) // 2
    return pl.pallas_call(
        functools.partial(attend_kernel, heads, groups, splits),
        in_specs=[pl.BlockSpec(memory_space=pltpu.SMEM), vmem, vmem],
        out_specs=[vmem] * 3,
        out_shape=[
            jax.ShapeDtypeStruct((groups, third, length), bf16),
            jax.ShapeDtypeStruct((groups, third, length), f32),
            jax.ShapeDtypeStruct((groups, 8, length), f32),
        ],
        scratch_shapes=[pltpu.VMEM((heads, blocks * length, dim), bf16), pltpu.VMEM((heads, dim, length), f32)],
        compiler_params=pltpu.CompilerParams(vmem_limit_bytes=vmem_bytes),
        cost_estimate=pl.CostEstimate(
            flops=units * length * length * 256 * 4,
            bytes_accessed=10 * 1024 * 1024,
            transcendentals=units * length * length,
        ),
        name="attend",
    )(own, qkv, tiles)


def attend_back_kernel(
    heads, groups, splits, own_ref, qkv_ref, bias_ref, grad_ref, wide_ref, lse_ref, normed_ref, weight_ref,
    gain_ref, named_ref, small_ref, q_ref, *refs,
):
    kv_refs, parts_ref = refs[:splits], refs[splits]
    diag_ref, sum_w, k3, v3, grad_k, grad_v, grad_q, grad_b = refs[splits + 1 :]
    length = bias_ref.shape[2]
    blocks = bias_ref.shape[1]
    dim = k3.shape[2]
    third = heads * dim
    for h in range(heads):

        def turn(c, _):
            start = pl.multiple_of(c * length, length)
            k3[h, pl.ds(start, length), :] = qkv_ref[
                third + h * dim : third + (h + 1) * dim, pl.ds(start, length)
            ].T
            v3[h, pl.ds(start, length), :] = qkv_ref[
                2 * third + h * dim : 2 * third + (h + 1) * dim, pl.ds(start, length)
            ].T
            grad_b[h, c] = jnp.zeros((length, length), f32)
            return 0

        lax.fori_loop(0, blocks, turn, 0)
    sum_w[...] = jnp.zeros_like(sum_w)
    grad_k[...] = jnp.zeros_like(grad_k)
    grad_v[...] = jnp.zeros_like(grad_v)
    own = own_ref[0]
    for j in range(groups):
        block = j * splits + own
        q_start = pl.multiple_of(block * length, length)
        grad_q[...] = jnp.zeros_like(grad_q)
        delta = []
        for h in range(heads):
            rows = slice(h * dim, (h + 1) * dim)
            delta.append(
                jnp.sum(grad_ref[j, rows, :].astype(f32) * wide_ref[j, rows, :], axis=0, keepdims=True)
            )

        def visit(c, state):
            start = pl.multiple_of(c * length, length)
            for h in range(heads):
                rows = slice(h * dim, (h + 1) * dim)
                q = qkv_ref[h * dim : (h + 1) * dim, pl.ds(q_start, length)]
                g = grad_ref[j, rows, :]
                s = dot_f32(k3[h, pl.ds(start, length), :], q, ((1,), (0,)))
                s = s + bias_ref[h, block - c].astype(f32)
                p = jnp.exp(s - lse_ref[j, h : h + 1, :])
                dp = dot_f32(v3[h, pl.ds(start, length), :], g, ((1,), (0,)))
                ds = (p * (dp - state[h])).astype(bf16)
                grad_v[rows, pl.ds(start, length)] += dot_f32(g, p.astype(bf16), ((1,), (1,)))
                grad_k[rows, pl.ds(start, length)] += dot_f32(q, ds, ((1,), (1,)))
                kt = qkv_ref[third + h * dim : third + (h + 1) * dim, pl.ds(start, length)]
                grad_q[rows, :] += dot_f32(kt, ds, ((1,), (0,)))
                grad_b[h, block - c] += ds.astype(f32)
            return state

        lax.fori_loop(0, block + 1, visit, tuple(delta))
        done = (grad_q[...] * 0.125).astype(bf16)
        q_ref[j] = done
        sum_w[:third, :] += dot_f32(done, normed_ref[block], ((1,), (0,)))
    for o in range(splits):
        other = jnp.bitwise_xor(own, o)
        for j in range(groups):
            start = pl.multiple_of((j * splits + other) * length, length)
            kv_refs[o][j, :third, :] = grad_k[:, pl.ds(start, length)].astype(bf16)
            kv_refs[o][j, third:, :] = grad_v[:, pl.ds(start, length)].astype(bf16)

    def weigh(c, _):
        start = pl.multiple_of(c * length, length)
        seen = normed_ref[c]
        sum_w[third : 2 * third, :] += dot_f32(grad_k[:, pl.ds(start, length)].astype(bf16), seen, ((1,), (0,)))
        sum_w[2 * third :, :] += dot_f32(grad_v[:, pl.ds(start, length)].astype(bf16), seen, ((1,), (0,)))
        return 0

    lax.fori_loop(0, blocks, weigh, 0)
    row = lax.broadcasted_iota(jnp.int32, (8, 2 * length), 0)

    def diagonals(d, _):
        for h in range(heads):
            tile = grad_b[h, d]
            tile = jnp.concatenate([jnp.zeros_like(tile), tile], axis=1)
            size = length // 2
            while size >= 8:
                tile = tile[:size] + pltpu.roll(tile[size:], 2 * length - size, 1)
                size //= 2
            for bit in (1, 2, 4):
                tile = jnp.where((row & bit) != 0, pltpu.roll(tile, 2 * length - bit, 1), tile)
            diag_ref[d, h : h + 1, :] = jnp.sum(tile, axis=0, keepdims=True)
        return 0

    lax.fori_loop(0, blocks, diagonals, 0)

    def by_bucket(d, total):
        start = pl.multiple_of(d * length, length)
        summed = diag_ref[d, :, length:]
        nearer = diag_ref[jnp.minimum(d + 1, blocks - 1), :, :length]
        summed = summed + jnp.where(d + 1 < blocks, 1.0, 0.0) * nearer
        return total + lax.dot_general(
            summed, named_ref[pl.ds(start, length), :], (((1,), (0,)), ((), ())),
            preferred_element_type=f32, precision=lax.Precision.HIGHEST,
        )

    diag_ref[:, heads:, :] = jnp.zeros((blocks, 8 - heads, 2 * length), f32)
    buckets = lax.fori_loop(0, blocks, by_bucket, jnp.zeros((8, named_ref.shape[1]), f32))
    made = sum_w[...]
    gain_grad = jnp.sum(made * weight_ref[...].astype(f32), axis=0, keepdims=True) / gain_ref[...]
    shares, small_rows, share = small_ref.shape
    size = 3 * third
    at = lax.broadcasted_iota(jnp.int32, (small_rows, share), 0)
    first_row = own_ref[1]
    each = named_ref.shape[1] // shares
    for d in range(shares):
        parts_ref[d, :size, :] = made[:, d * share : (d + 1) * share].astype(bf16)
        small = small_ref[d]
        small = small + jnp.where(at == own_ref[2], gain_grad[:, d * share : (d + 1) * share], 0.0)
        for h in range(heads):
            line = jnp.concatenate(
                [buckets[h : h + 1, d * each : (d + 1) * each], jnp.zeros((1, share - each), f32)], axis=1
            )
            small = small + jnp.where(at == first_row + h, line, 0.0)
        parts_ref[d, size:, :] = small.astype(bf16)


def attend_back(own, qkv, tiles, grad_context, wide, lse, normed, weight, gain, named, small, groups, splits):
    heads, blocks, length, _ = tiles.shape
    third = qkv.shape[0] // 3
    dim = third // heads
    vmem = pl.BlockSpec(memory_space=pltpu.VMEM)
    units = heads * groups * (blocks + 1) // 2
    shares, small_rows, share = small.shape
    return pl.pallas_call(
        functools.partial(attend_back_kernel, heads, groups, splits),
        in_specs=[pl.BlockSpec(memory_space=pltpu.SMEM)] + [vmem] * 10,
        out_specs=[vmem] * (2 + splits),
        out_shape=[jax.ShapeDtypeStruct((groups, third, length), bf16)]
        + [jax.ShapeDtypeStruct((groups, 2 * third, length), bf16)] * splits
        + [jax.ShapeDtypeStruct((shares, 3 * third + small_rows, share), bf16)],
        scratch_shapes=[
            pltpu.VMEM((blocks, 8, 2 * length), f32),
            pltpu.VMEM(weight.shape, f32),
            pltpu.VMEM((heads, blocks * length, dim), bf16),
            pltpu.VMEM((heads, blocks * length, dim), bf16),
            pltpu.VMEM((third, blocks * length), f32),
            pltpu.VMEM((third, blocks * length), f32),
            pltpu.VMEM((third, length), f32),
            pltpu.VMEM((heads, blocks, length, length), f32),
        ],
        compiler_params=pltpu.CompilerParams(vmem_limit_bytes=vmem_bytes),
        cost_estimate=pl.CostEstimate(
            flops=units * length * length * 256 * 10,
            bytes_accessed=20 * 1024 * 1024,
            transcendentals=units * length * length,
        ),
        name="attend_back",
    )(own, qkv, tiles, grad_context, wide, lse, normed, weight, gain, named, small)


def expert_kernel(
    experts, top, own_ref, xa_ref, xb_ref, ua_ref, ub_ref, router_ref, weight_ref,
    mixed_a, mixed_b, gx_a, gx_b, gg_a, gg_b, grad_ref, sum_rows, sum_gx, sum_grad, g_rows, gates,
):
    step = pl.program_id(0)
    near = xa_ref.shape[0]
    joined = weight_ref.shape[0]
    units = weight_ref.shape[1] // 2
    tile = min(near, 512)
    root = 0.7978845608028654
    places = [
        (half * near + at, half, slice(at, at + tile), slice(half * near + at, half * near + at + tile))
        for half in range(2)
        for at in range(0, near, tile)
    ]
    lane = lax.broadcasted_iota(jnp.int32, (tile, 128), 1)
    own = own_ref[0]

    @pl.when(step == 0)
    def _():
        sum_rows[...] = jnp.zeros_like(sum_rows)
        sum_gx[...] = jnp.zeros_like(sum_gx)
        for _, half, part, whole in places:
            x = (xa_ref, xb_ref)[half][part, :]
            width = x.shape[1]
            routes = (ua_ref, ub_ref)[half][part, width:].astype(jnp.int32)
            logits = dot_f32(x, router_ref[...], ((1,), (1,)))
            logits = jnp.where(lane < experts, logits, masked_score)
            chances = jnp.exp(logits - jnp.max(logits, axis=1, keepdims=True))
            chances = chances / jnp.sum(chances, axis=1, keepdims=True)
            select = jnp.zeros((tile, 128), f32)
            for k in range(top):
                select = select + jnp.where(lane == routes[:, k : k + 1], 1.0, 0.0)
            picked = select * chances
            mine = jnp.where(lane == own, 1.0, 0.0)
            gate = jnp.sum(mine * picked, axis=1, keepdims=True) / jnp.sum(picked, axis=1, keepdims=True)
            routed = jnp.sum(mine * select, axis=1, keepdims=True)
            gates[whole, :] = jnp.where(lane == 0, gate, routed)
            u = (ua_ref, ub_ref)[half][part, :width].astype(f32)
            g_rows[whole, :] = (gate * u).astype(bf16)

    first = jnp.concatenate([weight_ref[k, :units, :] for k in range(joined)], axis=0)
    second = jnp.concatenate([weight_ref[k, units:, :] for k in range(joined)], axis=0)
    cut = joined * units
    for start, half, part, whole in places:
        x = (xa_ref, xb_ref)[half][part, :]
        g = g_rows[whole, :]
        pre = dot_f32(x, first, ((1,), (1,)))
        back = dot_f32(g, second, ((1,), (1,)))
        square = pre * pre
        bent = jnp.tanh(pre * (root + (root * 0.044715) * square))
        halved = 0.5 + 0.5 * bent
        active = pre * halved
        hidden = active.astype(bf16)
        slope = halved + active * (1.0 - bent) * (root + (root * 0.134145) * square)
        gp = (back * slope).astype(bf16)
        sum_rows[whole, :] += dot_f32(hidden, second, ((1,), (0,)))
        sum_gx[whole, :] += dot_f32(gp, first, ((1,), (0,)))
        grad_first = dot_f32(gp, x, ((0,), (0,)))
        grad_second = dot_f32(hidden, g, ((0,), (0,)))
        if start == 0:
            sum_grad[:cut, :] = grad_first
            sum_grad[cut:, :] = grad_second
        else:
            sum_grad[:cut, :] += grad_first
            sum_grad[cut:, :] += grad_second
    for k in range(joined):
        grad_ref[k, :units, :] = sum_grad[k * units : (k + 1) * units, :].astype(bf16)
        grad_ref[k, units:, :] = sum_grad[cut + k * units : cut + (k + 1) * units, :].astype(bf16)

    @pl.when(step == pl.num_programs(0) - 1)
    def _():
        for _, half, part, whole in places:
            result = sum_rows[whole, :].astype(bf16).astype(f32)
            gate = gates[whole, 0:1]
            routed = gates[whole, 1:2]
            u = (ua_ref, ub_ref)[half][part, : result.shape[1]].astype(f32)
            dots = jnp.sum(u * result, axis=1, keepdims=True) * routed
            (gg_a, gg_b)[half][part, :] = jnp.where(lane == own, dots, 0.0)
            (mixed_a, mixed_b)[half][part, :] = (gate * result).astype(bf16)
            (gx_a, gx_b)[half][part, :] = jnp.where(routed > 0.5, sum_gx[whole, :], 0.0).astype(bf16)


def run_expert(own, x, u, router, experts, top, weights):
    rows, width = x[0].shape
    shards, units = weights.shape[0], weights.shape[1] // 2

    def whole(array):
        return pl.BlockSpec(array.shape, lambda i: (0, 0), pipeline_mode=pl.Buffered(1))

    def rows_of(columns):
        return pl.BlockSpec((rows, columns), lambda i: (0, 0))

    joined = 1
    shard_spec = pl.BlockSpec((joined, 2 * units, width), lambda i: (i, 0, 0))
    operands = (*x, *u, router)
    return pl.pallas_call(
        functools.partial(expert_kernel, experts, top),
        grid=(shards // joined,),
        in_specs=[pl.BlockSpec(memory_space=pltpu.SMEM)] + [whole(item) for item in operands] + [shard_spec],
        out_specs=[rows_of(width)] * 4 + [rows_of(128)] * 2 + [shard_spec],
        out_shape=[jax.ShapeDtypeStruct((rows, width), bf16)] * 4
        + [jax.ShapeDtypeStruct((rows, 128), f32)] * 2
        + [jax.ShapeDtypeStruct(weights.shape, bf16)],
        scratch_shapes=[pltpu.VMEM((2 * rows, width), f32)] * 2
        + [
            pltpu.VMEM((joined * 2 * units, width), f32),
            pltpu.VMEM((2 * rows, width), bf16),
            pltpu.VMEM((2 * rows, 128), f32),
        ],
        compiler_params=pltpu.CompilerParams(vmem_limit_bytes=vmem_bytes),
        cost_estimate=pl.CostEstimate(
            flops=24 * rows * width * units * shards,
            bytes_accessed=16 * rows * width + 8 * shards * width * units,
            transcendentals=2 * rows * units * shards,
        ),
        name="run_expert",
    )(own, *operands, weights)


def order_kernel(count, third, group_ref, *refs):
    held, (q_ref, k_ref, v_ref, small_ref), placed = refs[:count], refs[count : count + 4], refs[count + 4]
    share = q_ref.shape[0]
    group = group_ref[0]
    small = None
    for s in range(count):
        placed[(group + s) % count] = held[s][: 3 * third, :]
        term = held[s][3 * third :, :].astype(f32)
        small = term if small is None else small + term
    small_ref[...] = small
    row = lax.broadcasted_iota(jnp.int32, (share, share), 0)
    column = lax.broadcasted_iota(jnp.int32, (share, share), 1)
    unit = jnp.where(row == column, 1.0, 0.0).astype(bf16)
    for g in range(count):
        for k, out_ref in enumerate((q_ref, k_ref, v_ref)):
            turned = dot_f32(unit, placed[g, k * third : (k + 1) * third, :], ((1,), (1,)))
            out_ref[:, g * third : (g + 1) * third] = turned


def put_in_order(group, held, third):
    count = len(held)
    rows, share = held[0].shape
    vmem = pl.BlockSpec(memory_space=pltpu.VMEM)
    return pl.pallas_call(
        functools.partial(order_kernel, count, third),
        in_specs=[pl.BlockSpec(memory_space=pltpu.SMEM)] + [vmem] * count,
        out_specs=[vmem] * 4,
        out_shape=[jax.ShapeDtypeStruct((share, count * third), f32)] * 3
        + [jax.ShapeDtypeStruct((rows - 3 * third, share), f32)],
        scratch_shapes=[pltpu.VMEM((count, 3 * third, share), bf16)],
        compiler_params=pltpu.CompilerParams(vmem_limit_bytes=vmem_bytes),
        name="put_in_order",
    )(group, *held)


def norm_back(x, gain, grad):
    scale = lax.rsqrt(jnp.mean(x * x, axis=-1, keepdims=True) + eps_norm)
    weighted = grad * gain
    inner = jnp.mean(weighted * x, axis=-1, keepdims=True)
    return scale * weighted - x * (scale * scale * scale) * inner, jnp.sum(grad * x * scale, axis=0)


def body(
    tokens, cotangent, w_query, w_key, w_value, attention_output_weight, router, norm1_gain, norm2_gain,
    attn_bias, w_in, w_out, routes, buckets,
):
    n_ctx = lax.axis_size("ctx")
    n_dp = lax.axis_size("dp")
    ctx_at = lax.axis_index("ctx")
    dp_at = lax.axis_index("dp")
    half = n_ctx // 2
    _, length, width = tokens.shape
    all_heads = attn_bias.shape[1]
    bucket_count = attn_bias.shape[0] * n_dp
    experts = router.shape[1]
    groups = 4
    splits = n_ctx // groups
    heads = all_heads // groups
    dim = width // all_heads
    third = heads * dim
    group_at = ctx_at // splits
    split_at = ctx_at % splits
    rows_dp = w_query.shape[0]

    tok_same, tok_across = gather_ctx([tokens[0]])
    tokens_held = [entry[0] for entry in tok_same + tok_across]
    table_size = attn_bias.shape[0] * all_heads
    table_columns = -(-table_size // rows_dp)
    table = jnp.pad(attn_bias.reshape(-1), (0, table_columns * rows_dp - table_size)).reshape(table_columns, rows_dp).T
    behind = jnp.concatenate([router, norm1_gain[:, None], norm2_gain[:, None], table], axis=1)
    behind = jnp.pad(behind, ((0, 0), (0, 128 - behind.shape[1])))
    packed = jnp.concatenate([w_query, w_key, w_value, attention_output_weight, behind], axis=1)
    packed = in_order(gather_dp(packed, tok_same), dp_at)
    dense = jnp.concatenate([item[:, : 4 * width] for item in packed], axis=0)
    behind = jnp.concatenate([item[:, 4 * width :] for item in packed], axis=0)
    output_weight = dense[:, 3 * width :]
    own_columns = [
        lax.dynamic_slice_in_dim(dense, k * width + group_at * third, third, axis=1).T for k in range(3)
    ]
    qkv_weight = jnp.concatenate(own_columns, axis=0)
    small_t = behind.T
    router_weight = small_t[:experts]
    gain_first = small_t[experts : experts + 1].astype(f32)
    gain_second = small_t[experts + 1 : experts + 2].astype(f32)
    bias_table = small_t[experts + 2 : experts + 2 + table_columns].reshape(table_columns, n_dp, rows_dp)
    bias_table = bias_table.transpose(1, 0, 2).reshape(n_dp, -1)[:, :table_size].reshape(bucket_count, all_heads)

    units = w_in.shape[2]
    z_groups = [[2 * z + x for z in range(half)] for x in range(2)]
    expert_part, _ = lax.optimization_barrier((jnp.concatenate([w_in[0].T, w_out[0]], axis=0), tok_same))
    expert_weights = lax.all_gather(expert_part, "ctx", axis=0, axis_index_groups=z_groups)

    onehot = (buckets[:, None] == jnp.arange(bucket_count, dtype=jnp.int32)[None, :]).astype(bf16)
    bias_own = lax.dynamic_slice_in_dim(bias_table, group_at * heads, heads, axis=1)
    per_distance = dot_f32(bias_own, onehot, ((0,), (1,)))
    vec = jnp.concatenate([jnp.full((heads, length), masked_score, f32), per_distance], axis=1)
    vec = jnp.pad(vec, ((0, 8 - heads), (0, 0)))
    tiles = bias_tiles(vec, heads, n_ctx, length)

    z_at, x_at = ctx_at // 2, ctx_at % 2
    places = jnp.stack(
        [((z_at - s) % half) * 2 + x_at for s in range(half)]
        + [((z_at - s) % half) * 2 + (1 - x_at) for s in range(half)]
    ).astype(jnp.int32)
    qkv_weight, tiles = lax.optimization_barrier((qkv_weight, tiles))
    normed, qkv = project(tokens_held, places, gain_first, qkv_weight)
    upstream = jnp.pad(routes[0].astype(bf16), ((0, 0), (0, 128 - routes.shape[2])))
    upstream = jnp.concatenate([cotangent[0], upstream], axis=1)
    upstream, _ = lax.optimization_barrier((upstream, tok_same))
    own_split = split_at.astype(jnp.int32).reshape(1)
    low, wide, lse = attend(own_split, qkv, tiles, groups, splits)
    upstream_rows = gather_rows(upstream, qkv, low)
    index_groups = [[g * splits + b for g in range(groups)] for b in range(splits)]
    context_t = lax.all_to_all(
        low, "ctx", split_axis=0, concat_axis=0, tiled=True, axis_index_groups=index_groups
    ).reshape(width, length)
    context_t, upstream_rows = lax.optimization_barrier((context_t, upstream_rows))

    resid_in = tokens[0].astype(f32)
    residual = resid_in + dot_f32(context_t, output_weight, ((0,), (0,)))
    scale2 = lax.rsqrt(jnp.mean(residual * residual, axis=-1, keepdims=True) + eps_norm)
    second = (residual * scale2 * gain_second).astype(bf16)
    second_rows = gather_rows(second)

    def gate(rows, pairs):
        logits = dot_f32(rows, router_weight, ((1,), (1,)))
        shifted = jnp.exp(logits - jnp.max(logits, axis=-1, keepdims=True))
        chances = shifted / jnp.sum(shifted, axis=-1, keepdims=True)
        named = jnp.arange(experts, dtype=jnp.int32)[None, :]
        select = jnp.zeros(chances.shape, f32)
        for k in range(pairs.shape[1]):
            select = select + (pairs[:, k : k + 1] == named).astype(f32)
        total = jnp.sum(select * chances, axis=-1, keepdims=True)
        return chances, select, total

    own_expert = dp_at.astype(jnp.int32).reshape(1)
    router_wide = jnp.pad(router_weight, ((0, 128 - experts), (0, 0)))
    near = second_rows[0].shape[0]
    chunk = min(near, 1024)
    if chunk == near:
        made = run_expert(own_expert, second_rows, upstream_rows, router_wide, experts, routes.shape[2], expert_weights)
        grad_expert = made[6]
    else:

        def one_chunk(c, state):
            def cut(held):
                return lax.dynamic_slice_in_dim(held, c * chunk, chunk, axis=0)

            def put(held, new):
                return lax.dynamic_update_slice(held, new, (c * chunk, 0))

            made = run_expert(
                own_expert, [cut(v) for v in state[:2]], [cut(v) for v in state[2:4]], router_wide, experts,
                routes.shape[2], expert_weights,
            )
            high = [item.astype(bf16) for item in made[4:6]]
            low = [(item - h.astype(f32)).astype(bf16) for item, h in zip(made[4:6], high)]
            wide = [
                jnp.concatenate([m, h[:, :64], lo[:, :64]], axis=1) for m, h, lo in zip(made[0:2], high, low)
            ]
            order = (made[2], made[3], wide[0], wide[1])
            summed = (state[4].astype(f32) + made[6].astype(f32)).astype(bf16)
            return tuple(put(v, new) for v, new in zip(state[:4], order)) + (summed,)

        start = (*second_rows, *upstream_rows, jnp.zeros(expert_weights.shape, bf16))
        done = lax.fori_loop(0, near // chunk, one_chunk, start)
        made = [done[2][:, :width], done[3][:, :width], done[0], done[1]]
        made += [v[:, width : width + 64].astype(f32) + v[:, width + 64 :].astype(f32) for v in done[2:4]]
        grad_expert = done[4]
    mixed, grad_dispatched = made[0:2], made[2:4]
    grad_gate_rows = [item[:, :experts] for item in made[4:6]]
    grad_expert = lax.psum_scatter(
        grad_expert, "ctx", scatter_dimension=0, tiled=False, axis_index_groups=z_groups
    ).astype(f32)
    grad_w_in = grad_expert[:units].T[None]
    grad_w_out = grad_expert[units:][None]
    moe_grad = scatter_sum_end(*scatter_sum_rows(*grad_dispatched, bf16))
    grad_gating = scatter_sum_end(*scatter_sum_rows(*grad_gate_rows, f32))

    chances, select, total = gate(second, routes[0])
    inner = jnp.sum(select * grad_gating * chances, axis=-1, keepdims=True)
    grad_chances = select * (grad_gating / total - inner / (total * total))
    grad_logits = (chances * (grad_chances - jnp.sum(chances * grad_chances, axis=-1, keepdims=True))).astype(bf16)
    grad_router = dot_f32(grad_logits, second, ((0,), (0,)))
    grad_second = moe_grad + dot_f32(grad_logits, router_weight, ((1,), (0,)))
    grad_norm, grad_gain_second = norm_back(residual, gain_second, grad_second)
    grad_residual = cotangent[0].astype(f32) + grad_norm
    grad_attn = grad_residual.astype(bf16)

    mixed, _ = lax.optimization_barrier((mixed, grad_attn))
    layer_out = (residual + scatter_sum_end(*scatter_sum_rows(*mixed, bf16))).astype(bf16)[None]

    grad_context_t = dot_f32(output_weight, grad_attn, ((1,), (1,))).astype(bf16)
    grad_context = lax.all_to_all(
        grad_context_t.reshape(groups, third, length),
        "ctx", split_axis=0, concat_axis=0, tiled=True, axis_index_groups=index_groups,
    )
    grad_output_w = dot_f32(context_t, grad_attn, ((1,), (0,))).astype(bf16)

    def share_of(device):
        return lax.dynamic_slice_in_dim(grad_output_w, device * rows_dp, rows_dp, axis=0)

    shares = [share_of(dp_at)] + [xor_move(share_of(dp_at ^ o), "dp", o) for o in range(1, n_dp)]
    grad_output_w = sum(item.astype(f32) for item in shares)
    grad_context, grad_output_w = lax.optimization_barrier((grad_context, grad_output_w))
    small_count = experts + 2 + all_heads
    small = jnp.concatenate([grad_router, jnp.zeros((1, width), f32), grad_gain_second[None]], axis=0)
    small = jnp.pad(small.reshape(experts + 2, n_dp, rows_dp).transpose(1, 0, 2), ((0, 0), (0, -(experts + 2) % 32), (0, 0)))
    small = jnp.pad(small, ((0, 0), (0, -(-small_count // 32) * 32 - small.shape[1]), (0, 0)))
    mask = 1
    while mask < n_ctx:
        grad_output_w = grad_output_w + xor_move(grad_output_w.astype(bf16), "ctx", mask).astype(f32)
        mask *= 2
    numbers = jnp.stack([split_at, experts + 2 + group_at * heads, experts + 0 * split_at]).astype(jnp.int32)
    if n_ctx > 8:
        vec, _ = lax.optimization_barrier((vec, grad_attn))
        tiles = bias_tiles(vec, heads, n_ctx, length)
    made = attend_back(
        numbers, qkv, tiles, grad_context, wide, lse, normed, qkv_weight, gain_first, onehot.astype(f32), small,
        groups, splits,
    )
    grad_q, kept, parts = made[0], list(made[1 : 1 + splits]), made[1 + splits]

    mask = splits // 2
    while mask:
        arrived = [xor_move(item, "ctx", mask) for item in kept[mask:]]
        kept = [(mine.astype(f32) + other.astype(f32)).astype(bf16) for mine, other in zip(kept[:mask], arrived)]
        mask //= 2
    own_qkv = lax.all_to_all(
        jnp.concatenate([grad_q, kept[0]], axis=1),
        "ctx", split_axis=0, concat_axis=0, tiled=True, axis_index_groups=index_groups,
    )
    parts = lax.all_to_all(parts, "dp", split_axis=0, concat_axis=0, tiled=True)
    gw = jnp.sum(parts.astype(f32), axis=0)
    mask = 1
    while mask < splits:
        gw = gw + xor_move(gw.astype(bf16), "ctx", mask).astype(f32)
        mask *= 2
    gw = gw.astype(bf16)
    held = [gw] + [shift_move(gw, "ctx", -splits * s) for s in range(1, groups)]
    grad_wq, grad_wk, grad_wv, small_grads = put_in_order(group_at.astype(jnp.int32).reshape(1), held, third)
    grad_router = small_grads[:experts].T
    grad_gain_first = small_grads[experts]
    grad_gain_second = small_grads[experts + 1]
    grad_bias = small_grads[experts + 2 : small_count, : attn_bias.shape[0]].T

    grad_normed = None
    for k in range(3):
        part = own_qkv[:, k * third : (k + 1) * third, :].reshape(width, length)
        term = dot_f32(part, dense[:, k * width : (k + 1) * width], ((0,), (1,)))
        grad_normed = term if grad_normed is None else grad_normed + term
    grad_in_norm = norm_back(resid_in, gain_first, grad_normed)[0]
    input_grad = (grad_residual + grad_in_norm)[None]
    return (
        layer_out, input_grad, grad_wq, grad_wk, grad_wv, grad_output_w, grad_router,
        grad_gain_first, grad_gain_second, grad_bias, grad_w_in, grad_w_out,
    )


def solution(mesh):
    in_specs = (
        P("dp", "ctx", None),
        P("dp", "ctx", None),
        P("dp", None),
        P("dp", None),
        P("dp", None),
        P("dp", None),
        P("dp", None),
        P("dp"),
        P("dp"),
        P("dp", None),
        P("dp", None, "ctx"),
        P("dp", "ctx", None),
        P("dp", "ctx", None),
        P(),
    )
    out_specs = (
        P("dp", "ctx", None),
        P("dp", "ctx", None),
        P("dp", None),
        P("dp", None),
        P("dp", None),
        P("dp", None),
        P("dp", None),
        P("dp"),
        P("dp"),
        P("dp", None),
        P("dp", None, "ctx"),
        P("dp", "ctx", None),
    )
    return jax.shard_map(body, mesh=mesh, in_specs=in_specs, out_specs=out_specs, check_vma=False)
```
